128 devices in a mesh: ctx: 16 (over z, y), head: 8 (over x, core).
Axes of the slice: x: 4, y: 4, z: 4, core: 2. Of those that a mesh axis runs over, the one named last changes fastest.
Arguments:
- features: bfloat16 [16384, 16384], P('ctx', 'head'), may hold values from -6 to 6
- gates: bfloat16 [16384, 16384], P('ctx', 'head'), may hold values from -6 to 6
- state_io: bfloat16 [16384, 2, 2048], P('ctx', None, 'head'), may hold values from -6 to 6
- step_size: float32 [256, 16384], P('head', 'ctx'), may hold values from 0.004 to 0.02
- log_decay: float32 [256, 16384], P('head', 'ctx'), may hold values from -2 to 0, as said below
- conv_feat: bfloat16 [4, 16384], P(None, 'head'), may hold values from -3 to 3
- conv_state: bfloat16 [4, 2, 2048], P(None, None, 'head'), may hold values from -3 to 3
- skip_gain: float32 [256], P('head'), may hold values from 0.5 to 1.5
- norm_gain: float32 [16384], P('head'), may hold values from 0.25 to 1.75
Outputs:
- mixed: bfloat16 [16384, 16384], P(('ctx', 'head'))
The draws below stay inside these ranges and needn't reach their ends.
Inputs may be any that keep to these rules, and one draw needn't show every extreme that they name: `log_decay`: every entry is negative.
All inputs are finite; a program needn't handle non-finite values.
Results may differ from the reference program's by a relative error of at most 0.0034.
Values may be sent and summed in bfloat16 or wider, within the bound.
A program may use at most 256 MiB of HBM per device.

```python
import math
import jax
import jax.numpy as jnp
from jax import lax

MIXER_HEADS = 256
HEADDIM = 64
STATE = 256
GROUPS = 8
CONV = 4
SPAN = 128
TOK_DEV = 1024
INNER = 16384
RESPONSE_TOKENS = 16384


def draw_log_decay(key, part):
    random_split_keys = jax.random.split(key, 7)
    slow_share = 0.6
    slow_heads = jax.random.uniform(random_split_keys[0], (MIXER_HEADS, 1)) < slow_share
    fast_rate = jnp.exp(jax.random.uniform(random_split_keys[1], (MIXER_HEADS, 1), minval=math.log(0.02), maxval=math.log(0.035)))
    slow_rate = jnp.exp(jax.random.uniform(random_split_keys[2], (MIXER_HEADS, 1), minval=math.log(0.05), maxval=math.log(0.3))) / RESPONSE_TOKENS
    baseline_decay_rate = jnp.where(slow_heads, slow_rate, fast_rate)
    blocks = RESPONSE_TOKENS // TOK_DEV
    block_multiplier = jnp.exp(jax.random.uniform(random_split_keys[3], (MIXER_HEADS, blocks, 1), minval=math.log(0.5), maxval=math.log(2.0)))
    block_multiplier = jnp.broadcast_to(block_multiplier, (MIXER_HEADS, blocks, TOK_DEV)).reshape(MIXER_HEADS, RESPONSE_TOKENS)
    decay_jitter = jnp.exp(jax.random.uniform(random_split_keys[4], (MIXER_HEADS, RESPONSE_TOKENS), minval=-0.5, maxval=0.5))
    spike_position = jax.random.randint(random_split_keys[5], (3, 1), 0, RESPONSE_TOKENS)
    spike_decay_drop = jax.random.uniform(random_split_keys[6], (3, MIXER_HEADS, 1), minval=0.2, maxval=0.3)
    token_positions = jnp.arange(RESPONSE_TOKENS, dtype=jnp.int32)[None, :]
    decay_spikes = jnp.zeros((MIXER_HEADS, RESPONSE_TOKENS), jnp.float32)
    for spike_index in range(3):
        decay_spikes = decay_spikes + jnp.where(token_positions == spike_position[spike_index], jnp.log(1.0 - spike_decay_drop[spike_index]), 0.0)
    return (-baseline_decay_rate * block_multiplier * decay_jitter + decay_spikes).astype(jnp.float32)


def shard_levels(key, shape, cuts, low, top_value):
    gain, own = 1.0, jax.random.fold_in(key, 6)
    for dim, shards_of in cuts:
        steps = jnp.exp(jax.random.uniform(jax.random.fold_in(own, dim), (shards_of,), jnp.float32, low / len(cuts), top_value / len(cuts)))
        gain = gain * jnp.repeat(steps, shape[dim] // shards_of).reshape([-1 if axis == dim else 1 for axis in range(len(shape))])
    return gain


def bell_draw(stream_key, extent, deviation, limit, shards=(), kind=jnp.bfloat16):
    array = deviation * jax.random.normal(stream_key, extent, jnp.float32)
    if shards:
        array = array * shard_levels(stream_key, extent, shards, -0.22, 0.18)
    return jnp.clip(array, -limit, limit).astype(kind)


def setup_inputs(seed: int = 0) -> dict:
    arg_keys = jax.random.split(jax.random.key(seed), 10)
    return {
        "features": bell_draw(arg_keys[0], (RESPONSE_TOKENS, INNER), 1.0, 6.0, ((0, 16), (1, 8))),
        "gates": bell_draw(arg_keys[1], (RESPONSE_TOKENS, INNER), 1.0, 6.0, ((0, 16), (1, 8))),
        "state_io": bell_draw(arg_keys[2], (RESPONSE_TOKENS, 2, GROUPS * STATE), 1.0, 6.0, ((0, 16), (2, 8))),
        "step_size": jnp.clip(jnp.exp(math.log(0.02) - 1.6094378 * jax.random.uniform(arg_keys[3], (MIXER_HEADS, RESPONSE_TOKENS), jnp.float32) ** shard_levels(arg_keys[3], (MIXER_HEADS, RESPONSE_TOKENS), ((0, 8), (1, 16)), -0.2, 0.2)), 0.004, 0.02),
        "log_decay": draw_log_decay(jax.random.fold_in(arg_keys[9], 71), 0),
        "conv_feat": bell_draw(arg_keys[5], (CONV, INNER), CONV ** -0.5, 3.0, ((1, 8),)),
        "conv_state": bell_draw(arg_keys[6], (CONV, 2, GROUPS * STATE), CONV ** -0.5, 3.0, ((2, 8),)),
        "skip_gain": jnp.clip(0.5 + 1.0 * jax.random.uniform(arg_keys[7], (MIXER_HEADS,), jnp.float32) ** shard_levels(arg_keys[7], (MIXER_HEADS,), ((0, 8),), -0.2, 0.2), 0.5, 1.5),
        "norm_gain": jnp.clip(1.0 + 0.15 * jax.random.normal(arg_keys[8], (INNER,), jnp.float32), 0.25, 1.75),
    }


def causal_conv(values, kernel):
    taps = kernel.shape[0]
    length = values.shape[0]
    padding = [(taps - 1, 0)] + [(0, 0)] * (values.ndim - 1)
    padded = jnp.pad(values, padding)
    summed = jnp.zeros(values.shape, jnp.float32)
    for offset in range(taps):
        summed = summed + kernel[offset].astype(jnp.float32) * padded[offset:offset + length].astype(jnp.float32)
    return jax.nn.silu(summed).astype(jnp.bfloat16)

def group_scan(pieces):
    feat_group, in_group, out_group, step_group, decay_group = pieces
    span_count = RESPONSE_TOKENS // SPAN
    per_group = step_group.shape[0]
    feat_spans = feat_group.reshape(span_count, SPAN, per_group, HEADDIM)
    in_spans = in_group.reshape(span_count, SPAN, STATE)
    out_spans = out_group.reshape(span_count, SPAN, STATE)
    step_spans = step_group.reshape(per_group, span_count, SPAN).transpose(1, 0, 2)
    decay_spans = decay_group.reshape(per_group, span_count, SPAN).transpose(1, 0, 2)
    lower_mask = jnp.tril(jnp.ones((SPAN, SPAN), dtype=bool))

    def advance(carried, span):
        feats, in_maps, out_maps, steps, decays = span
        cumulated = jnp.cumsum(decays, axis=1)
        scores = jnp.dot(out_maps, in_maps.T, preferred_element_type=jnp.float32)
        gaps = cumulated[:, :, None] - cumulated[:, None, :]
        weights = (scores[None] * jnp.exp(jnp.where(lower_mask, gaps, -jnp.inf)) * steps[:, None, :]).astype(jnp.bfloat16)
        weights = lax.optimization_barrier(weights)
        output_diag = jnp.einsum('hts,shp->thp', weights.astype(jnp.float32), feats.astype(jnp.float32))
        state_low = lax.optimization_barrier(carried.astype(jnp.bfloat16))
        output_carried = jnp.einsum('tn,hpn->thp', out_maps.astype(jnp.float32), state_low.astype(jnp.float32)) * jnp.exp(cumulated).T[:, :, None]
        weighting = jnp.exp(cumulated[:, -1:] - cumulated) * steps
        scaled_in = (weighting.T[:, :, None] * feats.astype(jnp.float32)).astype(jnp.bfloat16)
        scaled_in = lax.optimization_barrier(scaled_in)
        local_state = jnp.einsum('shp,sn->hpn', scaled_in.astype(jnp.float32), in_maps.astype(jnp.float32))
        carried = jnp.exp(cumulated[:, -1])[:, None, None] * carried + local_state
        return (carried, output_diag + output_carried)
    zero_state = jnp.zeros((per_group, HEADDIM, STATE), jnp.float32)
    _, outputs = lax.scan(advance, zero_state, (feat_spans, in_spans, out_spans, step_spans, decay_spans))
    return outputs.reshape(RESPONSE_TOKENS, per_group, HEADDIM)

def reference(features, gates, state_io, step_size, log_decay, conv_feat, conv_state, skip_gain, norm_gain):
    per_group = MIXER_HEADS // GROUPS
    conv_out = causal_conv(features, conv_feat)
    conv_io = causal_conv(state_io, conv_state)
    feat_groups = conv_out.reshape(RESPONSE_TOKENS, GROUPS, per_group, HEADDIM).transpose(1, 0, 2, 3)
    in_groups = conv_io[:, 0].reshape(RESPONSE_TOKENS, GROUPS, STATE).transpose(1, 0, 2)
    out_groups = conv_io[:, 1].reshape(RESPONSE_TOKENS, GROUPS, STATE).transpose(1, 0, 2)
    step_groups = step_size.reshape(GROUPS, per_group, RESPONSE_TOKENS)
    decay_groups = log_decay.reshape(GROUPS, per_group, RESPONSE_TOKENS)
    state_out = lax.map(group_scan, (feat_groups, in_groups, out_groups, step_groups, decay_groups))
    state_out = state_out.transpose(1, 0, 2, 3).reshape(RESPONSE_TOKENS, INNER)
    skip_cols = jnp.repeat(skip_gain, HEADDIM)
    mixed_in = state_out + skip_cols[None, :] * conv_out.astype(jnp.float32)
    gated_out = mixed_in * jax.nn.silu(gates.astype(jnp.float32))
    grouped = gated_out.reshape(RESPONSE_TOKENS, GROUPS, INNER // GROUPS)
    mean_square = lax.optimization_barrier(jnp.mean(grouped * grouped, axis=2, keepdims=True))
    normed = (grouped * lax.rsqrt(mean_square + 1e-05)).reshape(RESPONSE_TOKENS, INNER) * norm_gain[None, :]
    return normed.astype(jnp.bfloat16)
```

```python
import functools

import jax
import jax.numpy as jnp
from jax import lax
from jax.experimental import pallas as pl
from jax.experimental.pallas import tpu as pltpu
from jax.sharding import PartitionSpec as P

F32 = jnp.float32
BF16 = jnp.bfloat16
MESH = pl.DeviceIdType.MESH

TOK = 1024
CH = 2048
HEADS = 32
HD = 64
ST = 256
GW = 256
NG = CH // GW
PER = GW // HD
L = 64
NCH = TOK // L
BLK = 128
NB = TOK // BLK
PAD = 16
TAPS = 4


def dot(a, b):
    return jnp.dot(a, b, preferred_element_type=F32)


def dot_nt(a, b):
    return lax.dot_general(a, b, (((1,), (1,)), ((), ())), preferred_element_type=F32)


def silu(v):
    half = 0.5 * v
    return half + half * jnp.tanh(half)


def split3(v):
    hi = v.astype(BF16)
    rest = v - hi.astype(F32)
    mid = rest.astype(BF16)
    low = (rest - mid.astype(F32)).astype(BF16)
    return hi, mid, low


def split_lanes(v):
    hi = v.astype(BF16).astype(F32)
    lane = lax.broadcasted_iota(jnp.int32, v.shape, 1)
    return jnp.where((lane // HEADS) % 2 == 0, hi, v - hi).astype(BF16)


def expander(piece, part):
    row = lax.broadcasted_iota(jnp.int32, (4 * HEADS, GW), 0)
    col = lax.broadcasted_iota(jnp.int32, (4 * HEADS, GW), 1)
    hit = (row % HEADS == PER * piece + col // HD) & (row // (2 * HEADS) == part)
    return jnp.where(hit, 1.0, 0.0).astype(BF16)


def mixer_kernel(
    nc,
    nh,
    feat_hbm,
    gate_hbm,
    sio_hbm,
    step_ref,
    decay_ref,
    cf_ref,
    cs_ref,
    sg_ref,
    z_out,
    rs_out,
    feat,
    gate,
    sio,
    xbuf,
    wx,
    in_rows,
    out_rows,
    in_t4,
    in_t,
    smask,
    fac_ab,
    fac_w,
    rows_fac,
    rows_g,
    shift,
    acc,
    carry,
    sbuf,
    gath,
    pbuf,
    inc,
    dsend,
    dall,
    zsend,
    rs_send,
    feat_sem,
    gate_sem,
    sio_sem,
    halo_send,
    halo_recv,
    d_send_sem,
    d_recv_sem,
    s_send,
    s_recv,
    p_send,
    p_recv,
    z_send,
    z_recv,
    r_send,
    r_recv,
):
    me = lax.axis_index("ctx")
    mh = lax.axis_index("head")
    sl = ST // nc
    tb = TOK // nh
    nxt = lax.rem(me + 1, nc)

    def rank(k):
        return lax.rem(me + k, nc)

    def peer(k):
        return lax.rem(mh + k, nh)

    def sio_in(i):
        return pltpu.make_async_copy(
            sio_hbm.at[i], sio.at[i, pl.ds(PAD, TOK)], sio_sem.at[i]
        )

    def feat_in(g):
        cols = pl.ds(pl.multiple_of(g * GW, GW), GW)
        return pltpu.make_async_copy(
            feat_hbm.at[:, cols], feat.at[g, pl.ds(PAD, TOK)], feat_sem.at[g]
        )

    def gate_in(g):
        cols = pl.ds(pl.multiple_of(g * GW, GW), GW)
        return pltpu.make_async_copy(gate_hbm.at[:, cols], gate.at[g], gate_sem.at[g])

    for i in range(2):
        sio_in(i).start()

    @pl.loop(0, NG)
    def _(g):
        feat_in(g).start()

    @pl.loop(0, NG)
    def _(g):
        gate_in(g).start()

    bar = pltpu.get_barrier_semaphore()

    @pl.loop(1, nc)
    def _(k):
        pl.semaphore_signal(bar, inc=1, device_id={"ctx": rank(k)}, device_id_type=MESH)

    @pl.loop(1, nh)
    def _(k):
        pl.semaphore_signal(bar, inc=1, device_id={"head": peer(k)}, device_id_type=MESH)

    pl.semaphore_wait(bar, nc - 1 + nh - 1)

    def halo_copy(g):
        cols = pl.ds(pl.multiple_of(g * GW, GW), GW)
        return pltpu.make_async_remote_copy(
            src_ref=feat_hbm.at[pl.ds(TOK - PAD, PAD), cols],
            dst_ref=feat.at[g, pl.ds(0, PAD)],
            send_sem=halo_send.at[g],
            recv_sem=halo_recv.at[g],
            device_id={"ctx": nxt},
            device_id_type=MESH,
        )

    def halo_map(i):
        return pltpu.make_async_remote_copy(
            src_ref=sio_hbm.at[i, pl.ds(TOK - PAD, PAD)],
            dst_ref=sio.at[i, pl.ds(0, PAD)],
            send_sem=halo_send.at[NG + i],
            recv_sem=halo_recv.at[NG + i],
            device_id={"ctx": nxt},
            device_id_type=MESH,
        )

    for i in range(2):
        halo_map(i).start()

    @pl.loop(0, NG)
    def _(g):
        halo_copy(g).start()

    def four(v):
        return jnp.concatenate([v, v, v, v], axis=0)

    decay3 = [four(p.astype(F32)).astype(BF16) for p in split3(decay_ref[...])]
    step3 = [four(p.astype(F32)).astype(BF16) for p in split3(step_ref[...])]

    row = lax.broadcasted_iota(jnp.int32, (64, TOK), 0)
    tok = lax.broadcasted_iota(jnp.int32, (64, TOK), 1)
    kind, unit = row // 16, row % 16
    in_chunk = tok // L == unit
    early = tok % L < L // 2
    hit = jnp.where(kind == 0, jnp.where(in_chunk & early, 1.0, 0.0), 0.0)
    hit = hit + jnp.where((kind == 1) & in_chunk, 1.0, 0.0)
    hit = hit + jnp.where((kind == 2) & in_chunk, jnp.where(early, 0.0, 1.0), 0.0)
    hit = hit + jnp.where((kind == 3) & (unit < 8), 1.0, 0.0)
    hit = hit + jnp.where((kind == 3) & (unit >= 8) & (tok // BLK > unit - 8), 1.0, 0.0)
    select = hit.astype(BF16)
    sums = dot_nt(select, decay3[0]) + dot_nt(select, decay3[1]) + dot_nt(select, decay3[2])
    rows_fac[...] = split_lanes(jnp.exp(sums[0:56]))

    r = lax.broadcasted_iota(jnp.int32, (BLK, BLK), 0)
    c = lax.broadcasted_iota(jnp.int32, (BLK, BLK), 1)
    eye = jnp.where(r == c, 1.0, 0.0).astype(BF16)
    after = jnp.where(c > r, 1.0, 0.0).astype(BF16)
    for b in range(NB):
        cut = slice(b * BLK, (b + 1) * BLK)
        suffix = sums[56 + b : 57 + b]
        steps = 0.0
        for d3, s3 in zip(decay3, step3):
            suffix = suffix + dot_nt(after, d3[:, cut])
            steps = steps + dot_nt(eye, s3[:, cut])
        fac_w[cut, :] = split_lanes(jnp.exp(suffix) * steps)

    for g in range(NG):
        spread = dot(rows_fac[48:56, :], expander(g, 0))
        dsend[0, :, g * GW : (g + 1) * GW] = spread[0:1]

    def d_copy(k):
        return pltpu.make_async_remote_copy(
            src_ref=dsend.at[0],
            dst_ref=dall.at[me],
            send_sem=d_send_sem,
            recv_sem=d_recv_sem,
            device_id={"ctx": rank(k)},
            device_id_type=MESH,
        )

    d_own = pltpu.make_async_copy(dsend.at[0], dall.at[me], d_recv_sem)
    d_own.start()

    @pl.loop(1, nc)
    def _(k):
        d_copy(k).start()

    sr = lax.broadcasted_iota(jnp.int32, (BLK, BLK + PAD), 0)
    sc = lax.broadcasted_iota(jnp.int32, (BLK, BLK + PAD), 1)
    for k in range(TAPS):
        shift[k] = jnp.where(sc == sr + PAD - TAPS + 1 + k, 1.0, 0.0).astype(BF16)

    def conv(block, taps):
        total = taps[0:1] * dot(shift[0], block)
        for k in range(1, TAPS):
            total = total + taps[k : k + 1] * dot(shift[k], block)
        return silu(total)

    def maps(i, store):
        sio_in(i).wait()
        halo_map(i).wait()

        @pl.when(me == 0)
        def _():
            sio[i, 0:PAD, :] = jnp.zeros((PAD, ST), BF16)

        taps = cs_ref[i]
        for b in range(NB):
            store(b, conv(sio[i, b * BLK : b * BLK + BLK + PAD, :], taps))

    def store_in(b, v):
        low = v.astype(BF16)
        in_rows[b * BLK : (b + 1) * BLK, :] = low
        turned = low.astype(F32).T.astype(BF16)
        in_t4[:, b * BLK : (b + 1) * BLK] = turned
        in_t[2 * b] = turned[:, 0:L]
        in_t[2 * b + 1] = turned[:, L : 2 * L]

    def store_out(b, v):
        out_rows[b * BLK : (b + 1) * BLK, :] = v.astype(BF16)

    maps(0, store_in)

    def s_copy(g, k):
        return pltpu.make_async_remote_copy(
            src_ref=sbuf.at[g, rank(k)],
            dst_ref=gath.at[g, me],
            send_sem=s_send.at[g],
            recv_sem=s_recv.at[g],
            device_id={"ctx": rank(k)},
            device_id_type=MESH,
        )

    def p_copy(g, k):
        return pltpu.make_async_remote_copy(
            src_ref=pbuf.at[g, rank(k)],
            dst_ref=inc.at[g, me],
            send_sem=p_send.at[g],
            recv_sem=p_recv.at[g],
            device_id={"ctx": rank(k)},
            device_id_type=MESH,
        )

    def z_copy(g, k):
        return pltpu.make_async_remote_copy(
            src_ref=zsend.at[g, peer(k)],
            dst_ref=z_out.at[g, mh],
            send_sem=z_send.at[g],
            recv_sem=z_recv.at[g],
            device_id={"head": peer(k)},
            device_id_type=MESH,
        )

    def phase_a(g):
        feat_in(g).wait()
        halo_copy(g).wait()

        @pl.when(me == 0)
        def _():
            feat[g, 0:PAD, :] = jnp.zeros((PAD, GW), BF16)

        spread = expander(g, 0)
        cols = pl.ds(pl.multiple_of(g * GW, GW), GW)
        taps = cf_ref[:, cols].astype(F32)

        @pl.loop(0, NB)
        def _(b):
            r0 = pl.multiple_of(b * BLK, BLK)
            x = conv(feat[g, pl.ds(r0, BLK + PAD), :], taps).astype(BF16)
            xbuf[g, pl.ds(r0, BLK), :] = x
            w = dot(fac_w[pl.ds(r0, BLK), :], spread)
            wx[pl.ds(r0, BLK), :] = (w * x.astype(F32)).astype(BF16)

        state = dot(in_t4[...], wx[...])
        sbuf[g] = state.astype(BF16).reshape(nc, sl, GW)
        pltpu.make_async_copy(sbuf.at[g, me], gath.at[g, me], s_recv.at[g]).start()

        @pl.loop(1, nc)
        def _(k):
            s_copy(g, k).start()

    def prepare_b():
        maps(1, store_out)
        inside = r // L == c // L
        mid = L // 2 - 1
        plus = inside & (c % L > mid) & (c <= r)
        minus = inside & (c % L <= mid) & (c > r)
        gap = (jnp.where(plus, 1.0, 0.0) - jnp.where(minus, 1.0, 0.0)).astype(BF16)
        lane = lax.broadcasted_iota(jnp.int32, (BLK, BLK), 1)
        for b in range(NB):
            cut = slice(b * BLK, (b + 1) * BLK)
            diff, steps = 0.0, 0.0
            for d3, s3 in zip(decay3, step3):
                diff = diff + dot_nt(gap, d3[:, cut])
                steps = steps + dot_nt(eye, s3[:, cut])
            first = lane < 2 * HEADS
            both = jnp.exp(jnp.where(first, diff, -diff)) * jnp.where(first, 1.0, steps)
            fac_ab[cut, :] = split_lanes(both)
        tr = lax.broadcasted_iota(jnp.int32, (L, L), 0)
        tc = lax.broadcasted_iota(jnp.int32, (L, L), 1)
        for n in range(NCH):
            cut = slice(n * L, (n + 1) * L)
            scores = dot_nt(out_rows[cut, :], in_rows[cut, :])
            smask[n] = jnp.where(tc <= tr, scores, 0.0).astype(BF16)
        acc[...] = jnp.zeros_like(acc)
        whole = dall.at[pl.ds(0, nc)]
        pltpu.make_async_copy(whole, whole, d_recv_sem).wait()

    def phase_x(g):
        pltpu.make_async_copy(gath.at[g], gath.at[g], s_recv.at[g]).wait()
        cols = pl.ds(pl.multiple_of(g * GW, GW), GW)
        running = jnp.zeros((sl, GW), F32)
        for q in range(nc):
            pbuf[g, q] = running.astype(BF16)
            running = dall[q, :, cols] * running + gath[g, q].astype(F32)
        pltpu.make_async_copy(pbuf.at[g, me], inc.at[g, me], p_recv.at[g]).start()

        @pl.loop(1, nc)
        def _(k):
            p_copy(g, k).start()

    def phase_b(g):
        gate_in(g).wait()
        pltpu.make_async_copy(inc.at[g], inc.at[g], p_recv.at[g]).wait()
        spread_a, spread_b = expander(g, 0), expander(g, 1)
        cols = pl.ds(pl.multiple_of(g * GW, GW), GW)
        skip = sg_ref[0:1, cols]
        gain = sg_ref[1:2, cols]
        rows_g[...] = dot(rows_fac[...], spread_a)
        carry[...] = inc[g].reshape(ST, GW).astype(F32)

        @pl.loop(0, NCH)
        def _(n):
            r0 = pl.multiple_of(n * L, L)
            fac = fac_ab[pl.ds(r0, L), :]
            x = xbuf[g, pl.ds(r0, L), :].astype(F32)
            bx = (dot(fac, spread_b) * x).astype(BF16)
            held = carry[...]
            low = (held * rows_g[pl.ds(n, 1), :]).astype(BF16)
            y = dot(smask[n], bx) + dot(out_rows[pl.ds(r0, L), :], low)
            carry[...] = held * rows_g[pl.ds(NCH + n, 1), :] + rows_g[
                pl.ds(2 * NCH + n, 1), :
            ] * dot(in_t[n], bx)
            mixed = dot(fac, spread_a) * y + skip * x
            gated = mixed * silu(gate[g, pl.ds(r0, L), :].astype(F32))
            square = gated * gated
            acc[pl.ds(r0, L), :] += square[:, 0:128] + square[:, 128:256]
            per = tb // L
            zsend[g, n // per, pl.ds(pl.multiple_of((n % per) * L, L), L), :] = (
                gated * gain
            ).astype(BF16)

        pltpu.make_async_copy(zsend.at[g, mh], z_out.at[g, mh], z_recv.at[g]).start()

        @pl.loop(1, nh)
        def _(k):
            z_copy(g, k).start()

    @pl.loop(0, NG + 2)
    def _(i):
        @pl.when(i < NG)
        def _():
            phase_a(i)

        @pl.when(i == 1)
        def _():
            prepare_b()

        @pl.when((i >= 1) & (i < NG + 1))
        def _():
            phase_x(i - 1)

        @pl.when(i >= 2)
        def _():
            phase_b(i - 2)

    for b in range(NB):
        flat = jnp.sum(acc[b * BLK : (b + 1) * BLK, :].T, axis=0, keepdims=True)
        unit, part = b * BLK // tb, b * BLK % tb
        rs_send[unit, :, part : part + BLK] = lax.rsqrt(flat * (1.0 / CH) + 1e-05)
    pltpu.make_async_copy(rs_send.at[mh], rs_out.at[mh], r_recv).start()

    def r_copy(k):
        return pltpu.make_async_remote_copy(
            src_ref=rs_send.at[peer(k)],
            dst_ref=rs_out.at[mh],
            send_sem=r_send,
            recv_sem=r_recv,
            device_id={"head": peer(k)},
            device_id_type=MESH,
        )

    @pl.loop(1, nh)
    def _(k):
        r_copy(k).start()

    some = dall.at[pl.ds(0, nc - 1)]
    pltpu.make_async_copy(some, some, d_send_sem).wait()

    @pl.loop(0, NG)
    def _(g):
        part = gath.at[g, pl.ds(0, nc - 1)]
        pltpu.make_async_copy(part, part, s_send.at[g]).wait()
        pltpu.make_async_copy(part, part, p_send.at[g]).wait()
        piece = zsend.at[g, pl.ds(0, nh - 1)]
        pltpu.make_async_copy(piece, piece, z_send.at[g]).wait()

    @pl.loop(0, NG)
    def _(g):
        pltpu.make_async_copy(zsend.at[g], zsend.at[g], z_recv.at[g]).wait()

    part = rs_send.at[pl.ds(0, nh - 1)]
    pltpu.make_async_copy(part, part, r_send).wait()
    pltpu.make_async_copy(rs_send, rs_send, r_recv).wait()


def mixer(nc, nh, features, gates, sio, step_size, log_decay, conv_feat, taps_io, sg):
    sl, tb = ST // nc, TOK // nh
    any_spec = pl.BlockSpec(memory_space=pl.ANY)
    vmem = pl.BlockSpec(memory_space=pltpu.VMEM)
    dma = pltpu.SemaphoreType.DMA
    return pl.pallas_call(
        functools.partial(mixer_kernel, nc, nh),
        out_shape=[
            jax.ShapeDtypeStruct((NG, nh, tb, GW), BF16),
            jax.ShapeDtypeStruct((nh, 1, tb), F32),
        ],
        in_specs=[any_spec] * 3 + [vmem] * 5,
        out_specs=[any_spec, any_spec],
        scratch_shapes=[
            pltpu.VMEM((NG, TOK + PAD, GW), BF16),
            pltpu.VMEM((NG, TOK, GW), BF16),
            pltpu.VMEM((2, TOK + PAD, ST), BF16),
            pltpu.VMEM((NG, TOK, GW), BF16),
            pltpu.VMEM((TOK, GW), BF16),
            pltpu.VMEM((TOK, ST), BF16),
            pltpu.VMEM((TOK, ST), BF16),
            pltpu.VMEM((ST, TOK), BF16),
            pltpu.VMEM((NCH, ST, L), BF16),
            pltpu.VMEM((NCH, L, L), BF16),
            pltpu.VMEM((TOK, 128), BF16),
            pltpu.VMEM((TOK, 128), BF16),
            pltpu.VMEM((56, 128), BF16),
            pltpu.VMEM((56, GW), F32),
            pltpu.VMEM((TAPS, BLK, BLK + PAD), BF16),
            pltpu.VMEM((TOK, 128), F32),
            pltpu.VMEM((ST, GW), F32),
            pltpu.VMEM((NG, nc, sl, GW), BF16),
            pltpu.VMEM((NG, nc, sl, GW), BF16),
            pltpu.VMEM((NG, nc, sl, GW), BF16),
            pltpu.VMEM((NG, nc, sl, GW), BF16),
            pltpu.VMEM((1, 1, CH), F32),
            pltpu.VMEM((nc, 1, CH), F32),
            pltpu.VMEM((NG, nh, tb, GW), BF16),
            pltpu.VMEM((nh, 1, tb), F32),
            dma((NG,)),
            dma((NG,)),
            dma((2,)),
            dma((NG + 2,)),
            dma((NG + 2,)),
            dma,
            dma,
            dma((NG,)),
            dma((NG,)),
            dma((NG,)),
            dma((NG,)),
            dma((NG,)),
            dma((NG,)),
            dma,
            dma,
        ],
        compiler_params=pltpu.CompilerParams(
            collective_id=0, has_side_effects=True, vmem_limit_bytes=52 << 20
        ),
        cost_estimate=pl.CostEstimate(
            flops=6_000_000_000, bytes_accessed=16_000_000, transcendentals=5_000_000
        ),
    )(features, gates, sio, step_size, log_decay, conv_feat, taps_io, sg)


def norm_kernel(z_ref, rs_ref, o_ref):
    tb = z_ref.shape[2]
    rows = jnp.broadcast_to(rs_ref[0], (128, tb))
    col = rows.T
    both = jnp.concatenate([col, col], axis=1)
    for g in range(NG):
        o_ref[:, g * GW : (g + 1) * GW] = (z_ref[g, 0].astype(F32) * both).astype(BF16)


def normalize(nh, z, rs):
    tb = TOK // nh
    return pl.pallas_call(
        norm_kernel,
        grid=(nh,),
        out_shape=jax.ShapeDtypeStruct((tb, nh * CH), BF16),
        in_specs=[
            pl.BlockSpec((NG, 1, tb, GW), lambda j: (0, j, 0, 0)),
            pl.BlockSpec((1, 1, tb), lambda j: (j, 0, 0)),
        ],
        out_specs=pl.BlockSpec((tb, CH), lambda j: (0, j)),
        cost_estimate=pl.CostEstimate(
            flops=4_000_000, bytes_accessed=8_400_000, transcendentals=0
        ),
    )(z, rs)


def shards(
    features, gates, state_io, step_size, log_decay, conv_feat, conv_state, skip_gain, norm_gain
):
    nc, nh = lax.axis_size("ctx"), lax.axis_size("head")
    sio = jnp.transpose(state_io, (1, 0, 2))
    taps_io = jnp.transpose(conv_state, (1, 0, 2)).astype(F32)
    sg = jnp.stack([jnp.repeat(skip_gain, HD), norm_gain])
    z, rs = mixer(nc, nh, features, gates, sio, step_size, log_decay, conv_feat, taps_io, sg)
    return normalize(nh, z, rs)


def solution(mesh):
    in_specs = (
        P("ctx", "head"),
        P("ctx", "head"),
        P("ctx", None, "head"),
        P("head", "ctx"),
        P("head", "ctx"),
        P(None, "head"),
        P(None, None, "head"),
        P("head"),
        P("head"),
    )
    out_specs = P(("ctx", "head"), None)
    return jax.shard_map(shards, mesh=mesh, in_specs=in_specs, out_specs=out_specs, check_vma=False)
```

```python
import functools

import jax
import jax.numpy as jnp
from jax import lax
from jax.experimental import pallas as pl
from jax.experimental.pallas import tpu as pltpu
from jax.sharding import PartitionSpec as P

F32 = jnp.float32
BF16 = jnp.bfloat16
MESH = pl.DeviceIdType.MESH

TOK = 1024
CH = 2048
HEADS = 32
HD = 64
ST = 256
GW = 256
NG = CH // GW
PER = GW // HD
L = 64
BLK = 128
NB = TOK // BLK
PAD = 16
TAPS = 4


def dot(a, b):
    return jnp.dot(a, b, preferred_element_type=F32)


def dot_nt(a, b):
    return lax.dot_general(a, b, (((1,), (1,)), ((), ())), preferred_element_type=F32)


def silu(v):
    half = 0.5 * v
    return half + half * jnp.tanh(half)


def split3(v):
    hi = v.astype(BF16)
    rest = v - hi.astype(F32)
    mid = rest.astype(BF16)
    low = (rest - mid.astype(F32)).astype(BF16)
    return hi, mid, low


def split_lanes(v):
    hi = v.astype(BF16).astype(F32)
    lane = lax.broadcasted_iota(jnp.int32, v.shape, 1)
    return jnp.where((lane // HEADS) % 2 == 0, hi, v - hi).astype(BF16)


def expander(piece, part):
    row = lax.broadcasted_iota(jnp.int32, (4 * HEADS, GW), 0)
    col = lax.broadcasted_iota(jnp.int32, (4 * HEADS, GW), 1)
    hit = (row % HEADS == PER * piece + col // HD) & (row // (2 * HEADS) == part)
    return jnp.where(hit, 1.0, 0.0).astype(BF16)


def mixer_kernel(
    nc,
    nh,
    feat_hbm,
    gate_hbm,
    sio_hbm,
    step_hbm,
    decay_hbm,
    cf_hbm,
    cs_hbm,
    skip_hbm,
    gain_hbm,
    z_out,
    rs_out,
    step_ref,
    decay_ref,
    cf_ref,
    cs_ref,
    skip_ref,
    gain_ref,
    skip_row,
    feat,
    gate,
    sio,
    xbuf,
    wx,
    in_rows,
    out_rows,
    in_t4,
    smask,
    fac_ab,
    fac_w,
    rows_fac,
    rows_g,
    shift,
    acc,
    carry,
    sbuf,
    gath,
    pbuf,
    inc,
    dsend,
    dall,
    zsend,
    rs_send,
    small_sem,
    feat_sem,
    gate_sem,
    sio_sem,
    halo_send,
    halo_recv,
    d_send_sem,
    d_recv_sem,
    s_send,
    s_recv,
    p_send,
    p_recv,
    z_send,
    z_recv,
    r_send,
    r_recv,
):
    me = lax.axis_index("ctx")
    mh = lax.axis_index("head")
    sl = ST // nc
    tb = TOK // nh
    nxt = lax.rem(me + 1, nc)

    def rank(k):
        return lax.rem(me + k, nc)

    def peer(k):
        return lax.rem(mh + k, nh)

    def sio_in(i):
        return pltpu.make_async_copy(
            sio_hbm.at[i], sio.at[i, pl.ds(PAD, TOK)], sio_sem.at[i]
        )

    def feat_in(g):
        cols = pl.ds(pl.multiple_of(g * GW, GW), GW)
        return pltpu.make_async_copy(
            feat_hbm.at[:, cols], feat.at[g, pl.ds(PAD, TOK)], feat_sem.at[g]
        )

    def gate_in(g):
        cols = pl.ds(pl.multiple_of(g * GW, GW), GW)
        return pltpu.make_async_copy(gate_hbm.at[:, cols], gate.at[g], gate_sem.at[g])

    small = [
        pltpu.make_async_copy(source, target, small_sem.at[i])
        for i, (source, target) in enumerate(
            [
                (decay_hbm, decay_ref),
                (step_hbm, step_ref),
                (cs_hbm, cs_ref),
                (cf_hbm, cf_ref),
                (skip_hbm, skip_ref),
                (gain_hbm, gain_ref),
            ]
        )
    ]
    for copy in small:
        copy.start()
    for i in range(2):
        sio_in(i).start()

    @pl.loop(0, NG)
    def _(g):
        feat_in(g).start()

    bar = pltpu.get_barrier_semaphore()

    @pl.loop(1, nc)
    def _(k):
        pl.semaphore_signal(bar, inc=1, device_id={"ctx": rank(k)}, device_id_type=MESH)

    @pl.loop(1, nh)
    def _(k):
        pl.semaphore_signal(bar, inc=1, device_id={"head": peer(k)}, device_id_type=MESH)

    for copy in small:
        copy.wait()

    def halo_copy(g):
        cols = pl.ds(pl.multiple_of(g * GW, GW), GW)
        return pltpu.make_async_remote_copy(
            src_ref=feat_hbm.at[pl.ds(TOK - PAD, PAD), cols],
            dst_ref=feat.at[g, pl.ds(0, PAD)],
            send_sem=halo_send.at[g],
            recv_sem=halo_recv.at[g],
            device_id={"ctx": nxt},
            device_id_type=MESH,
        )

    def halo_map(i):
        return pltpu.make_async_remote_copy(
            src_ref=sio_hbm.at[i, pl.ds(TOK - PAD, PAD)],
            dst_ref=sio.at[i, pl.ds(0, PAD)],
            send_sem=halo_send.at[NG + i],
            recv_sem=halo_recv.at[NG + i],
            device_id={"ctx": nxt},
            device_id_type=MESH,
        )

    def four(v):
        return jnp.concatenate([v, v, v, v], axis=0)

    decay3 = [four(p.astype(F32)).astype(BF16) for p in split3(decay_ref[...])]
    step3 = [four(p.astype(F32)).astype(BF16) for p in split3(step_ref[...])]

    row = lax.broadcasted_iota(jnp.int32, (64, TOK), 0)
    tok = lax.broadcasted_iota(jnp.int32, (64, TOK), 1)
    kind, unit = row // 8, row % 8
    chunk = row % 16
    late = tok % BLK >= L // 2 + L * (chunk % 2)
    own = tok // BLK == chunk // 2
    whole = tok // BLK == unit
    middle = (tok % BLK >= L // 2) & (tok % BLK < L // 2 + L)
    hit = jnp.where((kind < 2) & own, jnp.where(late, 0.0, 1.0), 0.0)
    hit = hit + jnp.where((kind >= 2) & (kind < 4) & own & late, 1.0, 0.0)
    hit = hit + jnp.where((kind == 4) & whole, 1.0, 0.0)
    hit = hit + jnp.where((kind == 5) & whole & middle, 1.0, 0.0)
    hit = hit + jnp.where(kind == 6, 1.0, 0.0)
    hit = hit + jnp.where((kind == 7) & (tok // BLK > unit), 1.0, 0.0)
    select = hit.astype(BF16)
    sums = dot_nt(select, decay3[0]) + dot_nt(select, decay3[1]) + dot_nt(select, decay3[2])
    rows_fac[...] = split_lanes(jnp.exp(sums[0:56]))

    r = lax.broadcasted_iota(jnp.int32, (BLK, BLK), 0)
    c = lax.broadcasted_iota(jnp.int32, (BLK, BLK), 1)
    eye = jnp.where(r == c, 1.0, 0.0).astype(BF16)
    after = jnp.where(c > r, 1.0, 0.0).astype(BF16)
    for b in range(NB):
        cut = slice(b * BLK, (b + 1) * BLK)
        suffix = sums[56 + b : 57 + b]
        steps = 0.0
        for d3, s3 in zip(decay3, step3):
            suffix = suffix + dot_nt(after, d3[:, cut])
            steps = steps + dot_nt(eye, s3[:, cut])
        fac_w[cut, :] = split_lanes(jnp.exp(suffix) * steps)

    head = lax.broadcasted_iota(jnp.int32, (HEADS, CH), 0)
    chan = lax.broadcasted_iota(jnp.int32, (HEADS, CH), 1)
    widen = jnp.where(chan // HD == head, 1.0, 0.0).astype(BF16)

    def widened(v):
        hi, mid, low = split3(v)
        return dot(hi, widen) + dot(mid, widen) + dot(low, widen)

    dsend[0] = widened(jnp.exp(sums[48:56, 0:HEADS]))[0:1]
    skip_row[...] = widened(jnp.broadcast_to(skip_ref[...], (8, HEADS)))[0:1]

    pl.semaphore_wait(bar, nc - 1 + nh - 1)
    for i in range(2):
        halo_map(i).start()

    @pl.loop(0, NG)
    def _(g):
        halo_copy(g).start()

    @pl.loop(0, NG)
    def _(g):
        gate_in(g).start()

    def d_copy(k):
        return pltpu.make_async_remote_copy(
            src_ref=dsend.at[0],
            dst_ref=dall.at[me],
            send_sem=d_send_sem,
            recv_sem=d_recv_sem,
            device_id={"ctx": rank(k)},
            device_id_type=MESH,
        )

    d_own = pltpu.make_async_copy(dsend.at[0], dall.at[me], d_recv_sem)
    d_own.start()

    @pl.loop(1, nc)
    def _(k):
        d_copy(k).start()

    sr = lax.broadcasted_iota(jnp.int32, (BLK, BLK + PAD), 0)
    sc = lax.broadcasted_iota(jnp.int32, (BLK, BLK + PAD), 1)
    for k in range(TAPS - 1):
        shift[k] = jnp.where(sc == sr + PAD - TAPS + 1 + k, 1.0, 0.0).astype(BF16)

    def conv(block, taps):
        total = taps[TAPS - 1 : TAPS] * block[PAD:, :].astype(F32)
        for k in range(TAPS - 1):
            total = total + taps[k : k + 1] * dot(shift[k], block)
        return silu(total)

    def maps(i, store):
        sio_in(i).wait()
        taps = cs_ref[...].astype(F32)[:, i]

        def one(b):
            store(b, conv(sio[i, b * BLK : b * BLK + BLK + PAD, :], taps))

        for b in range(1, NB):
            one(b)
        halo_map(i).wait()

        @pl.when(me == 0)
        def _():
            sio[i, 0:PAD, :] = jnp.zeros((PAD, ST), BF16)

        one(0)

    def store_in(b, v):
        low = v.astype(BF16)
        in_rows[b * BLK : (b + 1) * BLK, :] = low
        turned = low.astype(F32).T.astype(BF16)
        in_t4[:, b * BLK : (b + 1) * BLK] = turned

    def store_out(b, v):
        out_rows[b * BLK : (b + 1) * BLK, :] = v.astype(BF16)

    maps(0, store_in)

    def s_copy(g, k):
        return pltpu.make_async_remote_copy(
            src_ref=sbuf.at[g, rank(k)],
            dst_ref=gath.at[g, me],
            send_sem=s_send.at[g],
            recv_sem=s_recv.at[g],
            device_id={"ctx": rank(k)},
            device_id_type=MESH,
        )

    def p_copy(g, k):
        return pltpu.make_async_remote_copy(
            src_ref=pbuf.at[g, rank(k)],
            dst_ref=inc.at[g, me],
            send_sem=p_send.at[g],
            recv_sem=p_recv.at[g],
            device_id={"ctx": rank(k)},
            device_id_type=MESH,
        )

    def z_copy(g, k):
        return pltpu.make_async_remote_copy(
            src_ref=zsend.at[g, peer(k)],
            dst_ref=z_out.at[g, mh],
            send_sem=z_send.at[g],
            recv_sem=z_recv.at[g],
            device_id={"head": peer(k)},
            device_id_type=MESH,
        )

    def phase_a(g):
        feat_in(g).wait()
        spread = expander(g, 0)
        cols = pl.ds(pl.multiple_of(g * GW, GW), GW)
        taps = cf_ref[:, cols].astype(F32)

        def one(b):
            cut = slice(b * BLK, (b + 1) * BLK)
            x = conv(feat[g, b * BLK : b * BLK + BLK + PAD, :], taps).astype(BF16)
            xbuf[g, cut, :] = x
            wx[cut, :] = (dot(fac_w[cut, :], spread) * x.astype(F32)).astype(BF16)

        for b in range(1, NB):
            one(b)
        halo_copy(g).wait()

        @pl.when(me == 0)
        def _():
            feat[g, 0:PAD, :] = jnp.zeros((PAD, GW), BF16)

        one(0)
        state = dot(in_t4[...], wx[...])
        sbuf[g] = state.astype(BF16).reshape(nc, sl, GW)
        pltpu.make_async_copy(sbuf.at[g, me], gath.at[g, me], s_recv.at[g]).start()

        @pl.loop(1, nc)
        def _(k):
            s_copy(g, k).start()

    def prepare_b():
        maps(1, store_out)
        inside = r // L == c // L
        mid = L // 2 - 1
        plus = inside & (c % L > mid) & (c <= r)
        minus = inside & (c % L <= mid) & (c > r)
        gap = (jnp.where(plus, 1.0, 0.0) - jnp.where(minus, 1.0, 0.0)).astype(BF16)
        lane = lax.broadcasted_iota(jnp.int32, (BLK, BLK), 1)
        for b in range(NB):
            cut = slice(b * BLK, (b + 1) * BLK)
            diff, steps = 0.0, 0.0
            for d3, s3 in zip(decay3, step3):
                diff = diff + dot_nt(gap, d3[:, cut])
                steps = steps + dot_nt(eye, s3[:, cut])
            first = lane < 2 * HEADS
            both = jnp.exp(jnp.where(first, diff, -diff)) * jnp.where(first, 1.0, steps)
            fac_ab[cut, :] = split_lanes(both)
        for n in range(NB):
            cut = slice(n * BLK, (n + 1) * BLK)
            scores = dot_nt(out_rows[cut, :], in_rows[cut, :])
            smask[n] = jnp.where(c <= r, scores, 0.0).astype(BF16)
        acc[...] = jnp.zeros_like(acc)
        whole = dall.at[pl.ds(0, nc)]
        pltpu.make_async_copy(whole, whole, d_recv_sem).wait()

    def phase_x(g):
        pltpu.make_async_copy(gath.at[g], gath.at[g], s_recv.at[g]).wait()
        cols = pl.ds(pl.multiple_of(g * GW, GW), GW)
        running = jnp.zeros((sl, GW), F32)
        for q in range(nc):
            pbuf[g, q] = running.astype(BF16)
            running = dall[q, :, cols] * running + gath[g, q].astype(F32)
        pltpu.make_async_copy(pbuf.at[g, me], inc.at[g, me], p_recv.at[g]).start()

        @pl.loop(1, nc)
        def _(k):
            p_copy(g, k).start()

    def phase_b(g):
        gate_in(g).wait()
        pltpu.make_async_copy(inc.at[g], inc.at[g], p_recv.at[g]).wait()
        spread_a, spread_b = expander(g, 0), expander(g, 1)
        cols = pl.ds(pl.multiple_of(g * GW, GW), GW)
        skip = skip_row[:, cols]
        gain = gain_ref[:, cols]
        rows_g[...] = dot(rows_fac[...], spread_a)
        carry[...] = inc[g].reshape(ST, GW).astype(F32)

        @pl.loop(0, NB, unroll=2)
        def _(n):
            r0 = pl.multiple_of(n * BLK, BLK)

            def factor(i):
                return rows_g[pl.ds(i, 1), :]

            fac = fac_ab[pl.ds(r0, BLK), :]
            x = xbuf[g, pl.ds(r0, BLK), :].astype(F32)
            both = dot(fac, spread_b) * x
            early, late = both[0:L], both[L:BLK]
            to_late = jnp.concatenate([early * factor(40 + n), late], axis=0)
            to_end = jnp.concatenate(
                [early * factor(16 + 2 * n), late * factor(17 + 2 * n)], axis=0
            )
            held = carry[...]
            carried = dot(out_rows[pl.ds(r0, BLK), :], held.astype(BF16))
            added = dot(in_t4[:, pl.ds(r0, BLK)], to_end.astype(BF16))
            carry[...] = held * factor(32 + n) + added
            y = jnp.concatenate(
                [
                    dot(smask[n, 0:L, 0:L], early.astype(BF16)) + carried[0:L] * factor(2 * n),
                    dot(smask[n, L:BLK, :], to_late.astype(BF16))
                    + carried[L:BLK] * factor(2 * n + 1),
                ],
                axis=0,
            )
            mixed = dot(fac, spread_a) * y + skip * x
            gated = mixed * silu(gate[g, pl.ds(r0, BLK), :].astype(F32))
            square = gated * gated
            acc[pl.ds(r0, BLK), :] += square[:, 0:128] + square[:, 128:256]
            per = tb // BLK
            zsend[g, n // per, pl.ds(pl.multiple_of((n % per) * BLK, BLK), BLK), :] = (
                gated * gain
            ).astype(BF16)

        pltpu.make_async_copy(zsend.at[g, mh], z_out.at[g, mh], z_recv.at[g]).start()

        @pl.loop(1, nh)
        def _(k):
            z_copy(g, k).start()

    @pl.loop(0, NG + 2)
    def _(i):
        @pl.when(i < NG)
        def _():
            phase_a(i)

        @pl.when(i == 1)
        def _():
            prepare_b()

        @pl.when((i >= 1) & (i < NG + 1))
        def _():
            phase_x(i - 1)

        @pl.when(i >= 2)
        def _():
            phase_b(i - 2)

    for b in range(NB):
        flat = jnp.sum(acc[b * BLK : (b + 1) * BLK, :].T, axis=0, keepdims=True)
        unit, part = b * BLK // tb, b * BLK % tb
        rs_send[unit, :, part : part + BLK] = lax.rsqrt(flat * (1.0 / CH) + 1e-05)
    pltpu.make_async_copy(rs_send.at[mh], rs_out.at[mh], r_recv).start()

    def r_copy(k):
        return pltpu.make_async_remote_copy(
            src_ref=rs_send.at[peer(k)],
            dst_ref=rs_out.at[mh],
            send_sem=r_send,
            recv_sem=r_recv,
            device_id={"head": peer(k)},
            device_id_type=MESH,
        )

    @pl.loop(1, nh)
    def _(k):
        r_copy(k).start()

    some = dall.at[pl.ds(0, nc - 1)]
    pltpu.make_async_copy(some, some, d_send_sem).wait()

    @pl.loop(0, NG)
    def _(g):
        part = gath.at[g, pl.ds(0, nc - 1)]
        pltpu.make_async_copy(part, part, s_send.at[g]).wait()
        pltpu.make_async_copy(part, part, p_send.at[g]).wait()
        piece = zsend.at[g, pl.ds(0, nh - 1)]
        pltpu.make_async_copy(piece, piece, z_send.at[g]).wait()

    @pl.loop(0, NG)
    def _(g):
        pltpu.make_async_copy(zsend.at[g], zsend.at[g], z_recv.at[g]).wait()

    part = rs_send.at[pl.ds(0, nh - 1)]
    pltpu.make_async_copy(part, part, r_send).wait()
    pltpu.make_async_copy(rs_send, rs_send, r_recv).wait()


def mixer(nc, nh, *args):
    sl, tb = ST // nc, TOK // nh
    any_spec = pl.BlockSpec(memory_space=pl.ANY)
    hbm = pl.BlockSpec(memory_space=pltpu.HBM)
    dma = pltpu.SemaphoreType.DMA
    return pl.pallas_call(
        functools.partial(mixer_kernel, nc, nh),
        out_shape=[
            jax.ShapeDtypeStruct((NG, nh, tb, GW), BF16),
            jax.ShapeDtypeStruct((nh, 1, tb), F32),
        ],
        in_specs=[any_spec] * 3 + [hbm] * 6,
        out_specs=[any_spec, any_spec],
        scratch_shapes=[
            pltpu.VMEM((HEADS, TOK), F32),
            pltpu.VMEM((HEADS, TOK), F32),
            pltpu.VMEM((TAPS, CH), BF16),
            pltpu.VMEM((TAPS, 2, ST), BF16),
            pltpu.VMEM((1, HEADS), F32),
            pltpu.VMEM((1, CH), F32),
            pltpu.VMEM((1, CH), F32),
            pltpu.VMEM((NG, TOK + PAD, GW), BF16),
            pltpu.VMEM((NG, TOK, GW), BF16),
            pltpu.VMEM((2, TOK + PAD, ST), BF16),
            pltpu.VMEM((NG, TOK, GW), BF16),
            pltpu.VMEM((TOK, GW), BF16),
            pltpu.VMEM((TOK, ST), BF16),
            pltpu.VMEM((TOK, ST), BF16),
            pltpu.VMEM((ST, TOK), BF16),
            pltpu.VMEM((NB, BLK, BLK), BF16),
            pltpu.VMEM((TOK, 128), BF16),
            pltpu.VMEM((TOK, 128), BF16),
            pltpu.VMEM((56, 128), BF16),
            pltpu.VMEM((56, GW), F32),
            pltpu.VMEM((TAPS - 1, BLK, BLK + PAD), BF16),
            pltpu.VMEM((TOK, 128), F32),
            pltpu.VMEM((ST, GW), F32),
            pltpu.VMEM((NG, nc, sl, GW), BF16),
            pltpu.VMEM((NG, nc, sl, GW), BF16),
            pltpu.VMEM((NG, nc, sl, GW), BF16),
            pltpu.VMEM((NG, nc, sl, GW), BF16),
            pltpu.VMEM((1, 1, CH), F32),
            pltpu.VMEM((nc, 1, CH), F32),
            pltpu.VMEM((NG, nh, tb, GW), BF16),
            pltpu.VMEM((nh, 1, tb), F32),
            dma((6,)),
            dma((NG,)),
            dma((NG,)),
            dma((2,)),
            dma((NG + 2,)),
            dma((NG + 2,)),
            dma,
            dma,
            dma((NG,)),
            dma((NG,)),
            dma((NG,)),
            dma((NG,)),
            dma((NG,)),
            dma((NG,)),
            dma,
            dma,
        ],
        compiler_params=pltpu.CompilerParams(
            collective_id=0, has_side_effects=True, vmem_limit_bytes=56 << 20
        ),
        cost_estimate=pl.CostEstimate(
            flops=6_000_000_000, bytes_accessed=16_000_000, transcendentals=5_000_000
        ),
    )(*args)


def norm_kernel(z_hbm, rs_hbm, o_hbm, zin, rs, stage, in_sem, rs_sem, out_sem):
    nh, tb = z_hbm.shape[1], z_hbm.shape[2]

    def into(j):
        return pltpu.make_async_copy(z_hbm.at[:, j], zin.at[j], in_sem.at[j])

    def out(j):
        cols = pl.ds(pl.multiple_of(j * CH, CH), CH)
        return pltpu.make_async_copy(stage.at[j], o_hbm.at[:, cols], out_sem.at[j])

    factors = pltpu.make_async_copy(rs_hbm, rs, rs_sem)
    factors.start()

    @pl.loop(0, nh)
    def _(j):
        into(j).start()

    factors.wait()

    @pl.loop(0, nh)
    def _(j):
        col = jnp.broadcast_to(rs[j], (128, tb)).T
        into(j).wait()
        for g in range(NG):
            for half in range(GW // 128):
                low = half * 128
                z = zin[j, g, :, low : low + 128].astype(F32)
                stage[j, :, g * GW + low : g * GW + low + 128] = (z * col).astype(BF16)
        out(j).start()

    @pl.loop(0, nh)
    def _(j):
        out(j).wait()


def normalize(nh, z, rs):
    tb = TOK // nh
    hbm = pl.BlockSpec(memory_space=pltpu.HBM)
    dma = pltpu.SemaphoreType.DMA
    return pl.pallas_call(
        norm_kernel,
        out_shape=jax.ShapeDtypeStruct((tb, nh * CH), BF16),
        in_specs=[hbm, hbm],
        out_specs=hbm,
        scratch_shapes=[
            pltpu.VMEM((nh, NG, tb, GW), BF16),
            pltpu.VMEM((nh, 1, tb), F32),
            pltpu.VMEM((nh, tb, CH), BF16),
            dma((nh,)),
            dma,
            dma((nh,)),
        ],
        compiler_params=pltpu.CompilerParams(vmem_limit_bytes=56 << 20),
        cost_estimate=pl.CostEstimate(
            flops=4_000_000, bytes_accessed=8_400_000, transcendentals=0
        ),
    )(z, rs)


def shards(
    features, gates, state_io, step_size, log_decay, conv_feat, conv_state, skip_gain, norm_gain
):
    nc, nh = lax.axis_size("ctx"), lax.axis_size("head")
    sio = jnp.transpose(state_io, (1, 0, 2))
    z, rs = mixer(
        nc,
        nh,
        features,
        gates,
        sio,
        step_size,
        log_decay,
        conv_feat,
        conv_state,
        skip_gain.reshape(1, HEADS),
        norm_gain.reshape(1, CH),
    )
    return normalize(nh, z, rs)


def solution(mesh):
    in_specs = (
        P("ctx", "head"),
        P("ctx", "head"),
        P("ctx", None, "head"),
        P("head", "ctx"),
        P("head", "ctx"),
        P(None, "head"),
        P(None, None, "head"),
        P("head"),
        P("head"),
    )
    out_specs = P(("ctx", "head"), None)
    return jax.shard_map(shards, mesh=mesh, in_specs=in_specs, out_specs=out_specs, check_vma=False)
```

```python
import functools

import jax
import jax.numpy as jnp
from jax import lax
from jax.experimental import pallas as pl
from jax.experimental.pallas import tpu as pltpu
from jax.sharding import PartitionSpec as P

F32 = jnp.float32
BF16 = jnp.bfloat16
MESH = pl.DeviceIdType.MESH

TOK = 1024
CH = 2048
HEADS = 32
HD = 64
ST = 256
GW = 256
NG = CH // GW
PER = GW // HD
L = 64
BLK = 128
NB = TOK // BLK
PAD = 16
TAPS = 4


def dot(a, b):
    return jnp.dot(a, b, preferred_element_type=F32)


def dot_nt(a, b):
    return lax.dot_general(a, b, (((1,), (1,)), ((), ())), preferred_element_type=F32)


def silu(v):
    half = 0.5 * v
    return half + half * jnp.tanh(half)


def split3(v):
    hi = v.astype(BF16)
    rest = v - hi.astype(F32)
    mid = rest.astype(BF16)
    low = (rest - mid.astype(F32)).astype(BF16)
    return hi, mid, low


def split_lanes(v):
    hi = v.astype(BF16).astype(F32)
    lane = lax.broadcasted_iota(jnp.int32, v.shape, 1)
    return jnp.where((lane // HEADS) % 2 == 0, hi, v - hi).astype(BF16)


def expander(piece, part):
    row = lax.broadcasted_iota(jnp.int32, (4 * HEADS, GW), 0)
    col = lax.broadcasted_iota(jnp.int32, (4 * HEADS, GW), 1)
    hit = (row % HEADS == PER * piece + col // HD) & (row // (2 * HEADS) == part)
    return jnp.where(hit, 1.0, 0.0).astype(BF16)


def mixer_kernel(
    nc,
    nh,
    feat_hbm,
    gate_hbm,
    sio_hbm,
    step_hbm,
    decay_hbm,
    cf_hbm,
    cs_hbm,
    skip_hbm,
    gain_hbm,
    z_out,
    rs_out,
    step_ref,
    decay_ref,
    cf_ref,
    cs_ref,
    skip_ref,
    gain_ref,
    skip_row,
    feat,
    gate,
    sio,
    xbuf,
    wx,
    in_rows,
    out_rows,
    in_t4,
    smask,
    fac_ab,
    fac_w,
    rows_fac,
    rows_g,
    shift,
    acc,
    carry,
    sbuf,
    gath,
    pbuf,
    inc,
    dsend,
    dall,
    zsend,
    rs_send,
    small_sem,
    feat_sem,
    gate_sem,
    sio_sem,
    halo_send,
    halo_recv,
    d_send_sem,
    d_recv_sem,
    s_send,
    s_recv,
    p_send,
    p_recv,
    z_send,
    z_recv,
    r_send,
    r_recv,
):
    me = lax.axis_index("ctx")
    mh = lax.axis_index("head")
    sl = ST // nc
    tb = TOK // nh
    nxt = lax.rem(me + 1, nc)

    def rank(k):
        return lax.rem(me + k, nc)

    def peer(k):
        return lax.rem(mh + k, nh)

    sio_in = pltpu.make_async_copy(sio_hbm, sio.at[pl.ds(PAD, TOK)], sio_sem)

    def feat_in(g):
        cols = pl.ds(pl.multiple_of(g * GW, GW), GW)
        return pltpu.make_async_copy(
            feat_hbm.at[:, cols], feat.at[g, pl.ds(PAD, TOK)], feat_sem.at[g]
        )

    def gate_in(g):
        cols = pl.ds(pl.multiple_of(g * GW, GW), GW)
        return pltpu.make_async_copy(gate_hbm.at[:, cols], gate.at[g], gate_sem.at[g])

    small = [
        pltpu.make_async_copy(source, target, small_sem.at[i])
        for i, (source, target) in enumerate(
            [
                (decay_hbm, decay_ref),
                (step_hbm, step_ref),
                (cs_hbm, cs_ref),
                (cf_hbm, cf_ref),
                (skip_hbm, skip_ref),
                (gain_hbm, gain_ref),
            ]
        )
    ]
    for copy in small:
        copy.start()
    sio_in.start()

    @pl.loop(0, NG)
    def _(g):
        feat_in(g).start()

    bar = pltpu.get_barrier_semaphore()

    @pl.loop(1, nc, unroll=5)
    def _(k):
        pl.semaphore_signal(bar, inc=1, device_id={"ctx": rank(k)}, device_id_type=MESH)

    @pl.loop(1, nh, unroll=7)
    def _(k):
        pl.semaphore_signal(bar, inc=1, device_id={"head": peer(k)}, device_id_type=MESH)

    for copy in small:
        copy.wait()

    def halo_copy(g):
        cols = pl.ds(pl.multiple_of(g * GW, GW), GW)
        return pltpu.make_async_remote_copy(
            src_ref=feat_hbm.at[pl.ds(TOK - PAD, PAD), cols],
            dst_ref=feat.at[g, pl.ds(0, PAD)],
            send_sem=halo_send.at[g],
            recv_sem=halo_recv.at[g],
            device_id={"ctx": nxt},
            device_id_type=MESH,
        )

    halo_map = pltpu.make_async_remote_copy(
        src_ref=sio_hbm.at[pl.ds(TOK - PAD, PAD)],
        dst_ref=sio.at[pl.ds(0, PAD)],
        send_sem=halo_send.at[NG],
        recv_sem=halo_recv.at[NG],
        device_id={"ctx": nxt},
        device_id_type=MESH,
    )

    def four(v):
        return jnp.concatenate([v, v, v, v], axis=0)

    decay3 = [four(p.astype(F32)).astype(BF16) for p in split3(decay_ref[...])]
    step3 = [four(p.astype(F32)).astype(BF16) for p in split3(step_ref[...])]

    row = lax.broadcasted_iota(jnp.int32, (64, TOK), 0)
    tok = lax.broadcasted_iota(jnp.int32, (64, TOK), 1)
    kind, unit = row // 8, row % 8
    chunk = row % 16
    late = tok % BLK >= L // 2 + L * (chunk % 2)
    own = tok // BLK == chunk // 2
    whole = tok // BLK == unit
    middle = (tok % BLK >= L // 2) & (tok % BLK < L // 2 + L)
    hit = jnp.where((kind < 2) & own, jnp.where(late, 0.0, 1.0), 0.0)
    hit = hit + jnp.where((kind >= 2) & (kind < 4) & own & late, 1.0, 0.0)
    hit = hit + jnp.where((kind == 4) & whole, 1.0, 0.0)
    hit = hit + jnp.where((kind == 5) & whole & middle, 1.0, 0.0)
    hit = hit + jnp.where(kind == 6, 1.0, 0.0)
    hit = hit + jnp.where((kind == 7) & (tok // BLK > unit), 1.0, 0.0)
    select = hit.astype(BF16)
    sums = dot_nt(select, decay3[0]) + dot_nt(select, decay3[1]) + dot_nt(select, decay3[2])
    rows_fac[...] = split_lanes(jnp.exp(sums[0:56]))

    r = lax.broadcasted_iota(jnp.int32, (BLK, BLK), 0)
    c = lax.broadcasted_iota(jnp.int32, (BLK, BLK), 1)
    eye = jnp.where(r == c, 1.0, 0.0).astype(BF16)
    after = jnp.where(c > r, 1.0, 0.0).astype(BF16)
    for b in range(NB):
        cut = slice(b * BLK, (b + 1) * BLK)
        suffix = sums[56 + b : 57 + b]
        steps = 0.0
        for d3, s3 in zip(decay3, step3):
            suffix = suffix + dot_nt(after, d3[:, cut])
            steps = steps + dot_nt(eye, s3[:, cut])
        fac_w[cut, :] = split_lanes(jnp.exp(suffix) * steps)

    head = lax.broadcasted_iota(jnp.int32, (HEADS, CH), 0)
    chan = lax.broadcasted_iota(jnp.int32, (HEADS, CH), 1)
    widen = jnp.where(chan // HD == head, 1.0, 0.0).astype(BF16)

    def widened(v):
        hi, mid, low = split3(v)
        return dot(hi, widen) + dot(mid, widen) + dot(low, widen)

    dsend[0] = widened(jnp.exp(sums[48:56, 0:HEADS]))[0:1]
    skip_row[...] = widened(jnp.broadcast_to(skip_ref[...], (8, HEADS)))[0:1]

    pl.semaphore_wait(bar, nc - 1 + nh - 1)
    halo_map.start()

    @pl.loop(0, NG)
    def _(g):
        halo_copy(g).start()

    def d_copy(k):
        return pltpu.make_async_remote_copy(
            src_ref=dsend.at[0],
            dst_ref=dall.at[me],
            send_sem=d_send_sem,
            recv_sem=d_recv_sem,
            device_id={"ctx": rank(k)},
            device_id_type=MESH,
        )

    d_own = pltpu.make_async_copy(dsend.at[0], dall.at[me], d_recv_sem)
    d_own.start()

    @pl.loop(1, nc, unroll=5)
    def _(k):
        d_copy(k).start()

    sr = lax.broadcasted_iota(jnp.int32, (BLK, BLK + PAD), 0)
    sc = lax.broadcasted_iota(jnp.int32, (BLK, BLK + PAD), 1)
    for k in range(TAPS - 1):
        shift[k] = jnp.where(sc == sr + PAD - TAPS + 1 + k, 1.0, 0.0).astype(BF16)

    def conv(block, taps):
        total = taps[TAPS - 1 : TAPS] * block[PAD:, :].astype(F32)
        for k in range(TAPS - 1):
            total = total + taps[k : k + 1] * dot(shift[k], block)
        return silu(total)

    def maps(i, store, blocks):
        taps = cs_ref[...].astype(F32)[:, i]
        for b in blocks:
            store(b, conv(sio[b * BLK : b * BLK + BLK + PAD, i, :], taps))

    def store_in(b, v):
        low = v.astype(BF16)
        in_rows[b * BLK : (b + 1) * BLK, :] = low
        turned = low.astype(F32).T.astype(BF16)
        in_t4[:, b * BLK : (b + 1) * BLK] = turned

    def store_out(b, v):
        out_rows[b * BLK : (b + 1) * BLK, :] = v.astype(BF16)

    sio_in.wait()
    maps(0, store_in, range(1, NB))
    halo_map.wait()

    @pl.when(me == 0)
    def _():
        sio[0:PAD] = jnp.zeros((PAD, 2, ST), BF16)

    maps(0, store_in, range(1))

    def s_copy(g, k):
        return pltpu.make_async_remote_copy(
            src_ref=sbuf.at[g, rank(k)],
            dst_ref=gath.at[g, me],
            send_sem=s_send.at[g],
            recv_sem=s_recv.at[g],
            device_id={"ctx": rank(k)},
            device_id_type=MESH,
        )

    def p_copy(g, k):
        return pltpu.make_async_remote_copy(
            src_ref=pbuf.at[g, rank(k)],
            dst_ref=inc.at[g, me],
            send_sem=p_send.at[g],
            recv_sem=p_recv.at[g],
            device_id={"ctx": rank(k)},
            device_id_type=MESH,
        )

    def z_copy(g, k):
        return pltpu.make_async_remote_copy(
            src_ref=zsend.at[g, peer(k)],
            dst_ref=z_out.at[g, mh],
            send_sem=z_send.at[g],
            recv_sem=z_recv.at[g],
            device_id={"head": peer(k)},
            device_id_type=MESH,
        )

    def phase_a(g):
        feat_in(g).wait()
        spread = expander(g, 0)
        cols = pl.ds(pl.multiple_of(g * GW, GW), GW)
        taps = cf_ref[:, cols].astype(F32)

        def one(b):
            cut = slice(b * BLK, (b + 1) * BLK)
            x = conv(feat[g, b * BLK : b * BLK + BLK + PAD, :], taps).astype(BF16)
            xbuf[g, cut, :] = x
            wx[cut, :] = (dot(fac_w[cut, :], spread) * x.astype(F32)).astype(BF16)

        for b in range(1, NB):
            one(b)
        halo_copy(g).wait()

        @pl.when(me == 0)
        def _():
            feat[g, 0:PAD, :] = jnp.zeros((PAD, GW), BF16)

        one(0)
        state = dot(in_t4[...], wx[...])
        sbuf[g] = state.astype(BF16).reshape(nc, sl, GW)
        pltpu.make_async_copy(sbuf.at[g, me], gath.at[g, me], s_recv.at[g]).start()

        @pl.loop(1, nc, unroll=5)
        def _(k):
            s_copy(g, k).start()

    def prepare_b():
        maps(1, store_out, range(NB))
        inside = r // L == c // L
        mid = L // 2 - 1
        plus = inside & (c % L > mid) & (c <= r)
        minus = inside & (c % L <= mid) & (c > r)
        gap = (jnp.where(plus, 1.0, 0.0) - jnp.where(minus, 1.0, 0.0)).astype(BF16)
        lane = lax.broadcasted_iota(jnp.int32, (BLK, BLK), 1)
        for b in range(NB):
            cut = slice(b * BLK, (b + 1) * BLK)
            diff, steps = 0.0, 0.0
            for d3, s3 in zip(decay3, step3):
                diff = diff + dot_nt(gap, d3[:, cut])
                steps = steps + dot_nt(eye, s3[:, cut])
            first = lane < 2 * HEADS
            both = jnp.exp(jnp.where(first, diff, -diff)) * jnp.where(first, 1.0, steps)
            fac_ab[cut, :] = split_lanes(both)
        for n in range(NB):
            cut = slice(n * BLK, (n + 1) * BLK)
            scores = dot_nt(out_rows[cut, :], in_rows[cut, :])
            smask[n] = jnp.where(c <= r, scores, 0.0).astype(BF16)
        acc[...] = jnp.zeros_like(acc)
        whole = dall.at[pl.ds(0, nc)]
        pltpu.make_async_copy(whole, whole, d_recv_sem).wait()

    def phase_x(g):
        pltpu.make_async_copy(gath.at[g], gath.at[g], s_recv.at[g]).wait()
        cols = pl.ds(pl.multiple_of(g * GW, GW), GW)
        running = jnp.zeros((sl, GW), F32)
        for q in range(nc):
            pbuf[g, q] = running.astype(BF16)
            running = dall[q, :, cols] * running + gath[g, q].astype(F32)
        pltpu.make_async_copy(pbuf.at[g, me], inc.at[g, me], p_recv.at[g]).start()

        @pl.loop(1, nc, unroll=5)
        def _(k):
            p_copy(g, k).start()

    def phase_b(g):
        gate_in(g).wait()
        pltpu.make_async_copy(inc.at[g], inc.at[g], p_recv.at[g]).wait()
        spread_a, spread_b = expander(g, 0), expander(g, 1)
        cols = pl.ds(pl.multiple_of(g * GW, GW), GW)
        skip = skip_row[:, cols]
        gain = gain_ref[:, cols]
        rows_g[...] = dot(rows_fac[...], spread_a)
        carry[...] = inc[g].reshape(ST, GW).astype(F32)

        @pl.loop(0, NB, unroll=2)
        def _(n):
            r0 = pl.multiple_of(n * BLK, BLK)

            def factor(i):
                return rows_g[pl.ds(i, 1), :]

            fac = fac_ab[pl.ds(r0, BLK), :]
            x = xbuf[g, pl.ds(r0, BLK), :].astype(F32)
            both = dot(fac, spread_b) * x
            early, late = both[0:L], both[L:BLK]
            to_late = jnp.concatenate([early * factor(40 + n), late], axis=0)
            to_end = jnp.concatenate(
                [early * factor(16 + 2 * n), late * factor(17 + 2 * n)], axis=0
            )
            held = carry[...]
            carried = dot(out_rows[pl.ds(r0, BLK), :], held.astype(BF16))
            added = dot(in_t4[:, pl.ds(r0, BLK)], to_end.astype(BF16))
            carry[...] = held * factor(32 + n) + added
            y = jnp.concatenate(
                [
                    dot(smask[n, 0:L, 0:L], early.astype(BF16)) + carried[0:L] * factor(2 * n),
                    dot(smask[n, L:BLK, :], to_late.astype(BF16))
                    + carried[L:BLK] * factor(2 * n + 1),
                ],
                axis=0,
            )
            mixed = dot(fac, spread_a) * y + skip * x
            gated = mixed * silu(gate[g, pl.ds(r0, BLK), :].astype(F32))
            square = gated * gated
            acc[pl.ds(r0, BLK), :] += square[:, 0:128] + square[:, 128:256]
            per = tb // BLK
            zsend[g, n // per, pl.ds(pl.multiple_of((n % per) * BLK, BLK), BLK), :] = (
                gated * gain
            ).astype(BF16)

        pltpu.make_async_copy(zsend.at[g, mh], z_out.at[g, mh], z_recv.at[g]).start()

        @pl.loop(1, nh, unroll=7)
        def _(k):
            z_copy(g, k).start()

    def states_by(i):
        return jnp.clip(jnp.maximum(i + 1, 2 * i - 1), 0, NG)

    def prefixes_by(i):
        return jnp.clip(jnp.maximum(i, 2 * i - 3), 0, NG)

    @pl.loop(0, NG + 2)
    def _(i):
        pl.loop(states_by(i - 1), states_by(i))(phase_a)

        @pl.when(i == 1)
        def _():
            @pl.loop(0, NG)
            def _(g):
                gate_in(g).start()

            prepare_b()

        pl.loop(prefixes_by(i - 1), prefixes_by(i))(phase_x)

        @pl.when(i >= 2)
        def _():
            phase_b(i - 2)

    for b in range(NB):
        flat = jnp.sum(acc[b * BLK : (b + 1) * BLK, :].T, axis=0, keepdims=True)
        unit, part = b * BLK // tb, b * BLK % tb
        rs_send[unit, :, part : part + BLK] = lax.rsqrt(flat * (1.0 / CH) + 1e-05)
    pltpu.make_async_copy(rs_send.at[mh], rs_out.at[mh], r_recv).start()

    def r_copy(k):
        return pltpu.make_async_remote_copy(
            src_ref=rs_send.at[peer(k)],
            dst_ref=rs_out.at[mh],
            send_sem=r_send,
            recv_sem=r_recv,
            device_id={"head": peer(k)},
            device_id_type=MESH,
        )

    @pl.loop(1, nh, unroll=7)
    def _(k):
        r_copy(k).start()

    some = dall.at[pl.ds(0, nc - 1)]
    pltpu.make_async_copy(some, some, d_send_sem).wait()

    @pl.loop(0, NG)
    def _(g):
        part = gath.at[g, pl.ds(0, nc - 1)]
        pltpu.make_async_copy(part, part, s_send.at[g]).wait()
        pltpu.make_async_copy(part, part, p_send.at[g]).wait()
        piece = zsend.at[g, pl.ds(0, nh - 1)]
        pltpu.make_async_copy(piece, piece, z_send.at[g]).wait()

    @pl.loop(0, NG)
    def _(g):
        pltpu.make_async_copy(zsend.at[g], zsend.at[g], z_recv.at[g]).wait()

    part = rs_send.at[pl.ds(0, nh - 1)]
    pltpu.make_async_copy(part, part, r_send).wait()
    pltpu.make_async_copy(rs_send, rs_send, r_recv).wait()


def mixer(nc, nh, *args):
    sl, tb = ST // nc, TOK // nh
    any_spec = pl.BlockSpec(memory_space=pl.ANY)
    hbm = pl.BlockSpec(memory_space=pltpu.HBM)
    dma = pltpu.SemaphoreType.DMA
    return pl.pallas_call(
        functools.partial(mixer_kernel, nc, nh),
        out_shape=[
            jax.ShapeDtypeStruct((NG, nh, tb, GW), BF16),
            jax.ShapeDtypeStruct((nh, 1, tb), F32),
        ],
        in_specs=[any_spec] * 3 + [hbm] * 6,
        out_specs=[any_spec, any_spec],
        scratch_shapes=[
            pltpu.VMEM((HEADS, TOK), F32),
            pltpu.VMEM((HEADS, TOK), F32),
            pltpu.VMEM((TAPS, CH), BF16),
            pltpu.VMEM((TAPS, 2, ST), BF16),
            pltpu.VMEM((1, HEADS), F32),
            pltpu.VMEM((1, CH), F32),
            pltpu.VMEM((1, CH), F32),
            pltpu.VMEM((NG, TOK + PAD, GW), BF16),
            pltpu.VMEM((NG, TOK, GW), BF16),
            pltpu.VMEM((TOK + PAD, 2, ST), BF16),
            pltpu.VMEM((NG, TOK, GW), BF16),
            pltpu.VMEM((TOK, GW), BF16),
            pltpu.VMEM((TOK, ST), BF16),
            pltpu.VMEM((TOK, ST), BF16),
            pltpu.VMEM((ST, TOK), BF16),
            pltpu.VMEM((NB, BLK, BLK), BF16),
            pltpu.VMEM((TOK, 128), BF16),
            pltpu.VMEM((TOK, 128), BF16),
            pltpu.VMEM((56, 128), BF16),
            pltpu.VMEM((56, GW), F32),
            pltpu.VMEM((TAPS - 1, BLK, BLK + PAD), BF16),
            pltpu.VMEM((TOK, 128), F32),
            pltpu.VMEM((ST, GW), F32),
            pltpu.VMEM((NG, nc, sl, GW), BF16),
            pltpu.VMEM((NG, nc, sl, GW), BF16),
            pltpu.VMEM((NG, nc, sl, GW), BF16),
            pltpu.VMEM((NG, nc, sl, GW), BF16),
            pltpu.VMEM((1, 1, CH), F32),
            pltpu.VMEM((nc, 1, CH), F32),
            pltpu.VMEM((NG, nh, tb, GW), BF16),
            pltpu.VMEM((nh, 1, tb), F32),
            dma((6,)),
            dma((NG,)),
            dma((NG,)),
            dma,
            dma((NG + 1,)),
            dma((NG + 1,)),
            dma,
            dma,
            dma((NG,)),
            dma((NG,)),
            dma((NG,)),
            dma((NG,)),
            dma((NG,)),
            dma((NG,)),
            dma,
            dma,
        ],
        compiler_params=pltpu.CompilerParams(
            collective_id=0, has_side_effects=True, vmem_limit_bytes=56 << 20
        ),
        cost_estimate=pl.CostEstimate(
            flops=6_000_000_000, bytes_accessed=16_000_000, transcendentals=5_000_000
        ),
    )(*args)


def norm_kernel(z_hbm, rs_hbm, o_hbm, zin, rs, stage, in_sem, rs_sem, out_sem):
    nh, tb = z_hbm.shape[1], z_hbm.shape[2]

    def into(j):
        return pltpu.make_async_copy(z_hbm.at[:, j], zin.at[j], in_sem.at[j])

    def out(j):
        cols = pl.ds(pl.multiple_of(j * CH, CH), CH)
        return pltpu.make_async_copy(stage.at[j], o_hbm.at[:, cols], out_sem.at[j])

    factors = pltpu.make_async_copy(rs_hbm, rs, rs_sem)
    factors.start()

    @pl.loop(0, nh)
    def _(j):
        into(j).start()

    factors.wait()

    @pl.loop(0, nh)
    def _(j):
        col = jnp.broadcast_to(rs[j], (128, tb)).T
        into(j).wait()
        for g in range(NG):
            for half in range(GW // 128):
                low = half * 128
                z = zin[j, g, :, low : low + 128].astype(F32)
                stage[j, :, g * GW + low : g * GW + low + 128] = (z * col).astype(BF16)
        out(j).start()

    @pl.loop(0, nh)
    def _(j):
        out(j).wait()


def normalize(nh, z, rs):
    tb = TOK // nh
    hbm = pl.BlockSpec(memory_space=pltpu.HBM)
    dma = pltpu.SemaphoreType.DMA
    return pl.pallas_call(
        norm_kernel,
        out_shape=jax.ShapeDtypeStruct((tb, nh * CH), BF16),
        in_specs=[hbm, hbm],
        out_specs=hbm,
        scratch_shapes=[
            pltpu.VMEM((nh, NG, tb, GW), BF16),
            pltpu.VMEM((nh, 1, tb), F32),
            pltpu.VMEM((nh, tb, CH), BF16),
            dma((nh,)),
            dma,
            dma((nh,)),
        ],
        compiler_params=pltpu.CompilerParams(vmem_limit_bytes=56 << 20),
        cost_estimate=pl.CostEstimate(
            flops=4_000_000, bytes_accessed=8_400_000, transcendentals=0
        ),
    )(z, rs)


def shards(
    features, gates, state_io, step_size, log_decay, conv_feat, conv_state, skip_gain, norm_gain
):
    nc, nh = lax.axis_size("ctx"), lax.axis_size("head")
    z, rs = mixer(
        nc,
        nh,
        features,
        gates,
        state_io,
        step_size,
        log_decay,
        conv_feat,
        conv_state,
        skip_gain.reshape(1, HEADS),
        norm_gain.reshape(1, CH),
    )
    return normalize(nh, z, rs)


def solution(mesh):
    in_specs = (
        P("ctx", "head"),
        P("ctx", "head"),
        P("ctx", None, "head"),
        P("head", "ctx"),
        P("head", "ctx"),
        P(None, "head"),
        P(None, None, "head"),
        P("head"),
        P("head"),
    )
    out_specs = P(("ctx", "head"), None)
    return jax.shard_map(shards, mesh=mesh, in_specs=in_specs, out_specs=out_specs, check_vma=False)
```

```python
import functools

import jax
import jax.numpy as jnp
from jax import lax
from jax.experimental import pallas as pl
from jax.experimental.pallas import tpu as pltpu
from jax.sharding import PartitionSpec as P

F32 = jnp.float32
BF16 = jnp.bfloat16
MESH = pl.DeviceIdType.MESH

TOK = 1024
CH = 2048
HEADS = 32
HD = 64
ST = 256
GW = 256
NG = CH // GW
PER = GW // HD
L = 64
BLK = 128
NB = TOK // BLK
PAD = 16
TAPS = 4


def dot(a, b):
    return jnp.dot(a, b, preferred_element_type=F32)


def dot_nt(a, b):
    return lax.dot_general(a, b, (((1,), (1,)), ((), ())), preferred_element_type=F32)


def silu(v):
    half = 0.5 * v
    return half + half * jnp.tanh(half)


def split3(v):
    hi = v.astype(BF16)
    rest = v - hi.astype(F32)
    mid = rest.astype(BF16)
    low = (rest - mid.astype(F32)).astype(BF16)
    return hi, mid, low


def split_lanes(v):
    hi = v.astype(BF16).astype(F32)
    lane = lax.broadcasted_iota(jnp.int32, v.shape, 1)
    return jnp.where((lane // HEADS) % 2 == 0, hi, v - hi).astype(BF16)


def expander(piece, part):
    row = lax.broadcasted_iota(jnp.int32, (4 * HEADS, GW), 0)
    col = lax.broadcasted_iota(jnp.int32, (4 * HEADS, GW), 1)
    hit = (row % HEADS == PER * piece + col // HD) & (row // (2 * HEADS) == part)
    return jnp.where(hit, 1.0, 0.0).astype(BF16)


def mixer_kernel(
    nc,
    nh,
    feat_hbm,
    gate_hbm,
    sio_hbm,
    step_hbm,
    decay_hbm,
    cf_hbm,
    cs_hbm,
    skip_hbm,
    gain_hbm,
    z_out,
    rs_out,
    step_ref,
    decay_ref,
    cf_ref,
    cs_ref,
    skip_ref,
    gain_ref,
    skip_row,
    feat,
    gate,
    sio,
    xbuf,
    wx,
    in_rows,
    out_rows,
    in_t4,
    smask,
    fac_ab,
    fac_w,
    rows_fac,
    rows_g,
    shift,
    acc,
    carry,
    sbuf,
    gath,
    pbuf,
    inc,
    dsend,
    dall,
    zsend,
    rs_send,
    small_sem,
    feat_sem,
    gate_sem,
    sio_sem,
    halo_send,
    halo_recv,
    d_send_sem,
    d_recv_sem,
    s_send,
    s_recv,
    p_send,
    p_recv,
    z_send,
    z_recv,
    r_send,
    r_recv,
):
    me = lax.axis_index("ctx")
    mh = lax.axis_index("head")
    sl = ST // nc
    tb = TOK // nh
    nxt = lax.rem(me + 1, nc)

    def rank(k):
        return lax.rem(me + k, nc)

    def peer(k):
        return lax.rem(mh + k, nh)

    sio_in = pltpu.make_async_copy(sio_hbm, sio.at[pl.ds(PAD, TOK)], sio_sem)

    def feat_in(g):
        cols = pl.ds(pl.multiple_of(g * GW, GW), GW)
        return pltpu.make_async_copy(
            feat_hbm.at[:, cols], feat.at[g, pl.ds(PAD, TOK)], feat_sem.at[g]
        )

    def gate_in(g):
        cols = pl.ds(pl.multiple_of(g * GW, GW), GW)
        return pltpu.make_async_copy(gate_hbm.at[:, cols], gate.at[g], gate_sem.at[g])

    small = [
        pltpu.make_async_copy(source, target, small_sem.at[i])
        for i, (source, target) in enumerate(
            [
                (decay_hbm, decay_ref),
                (step_hbm, step_ref),
                (cs_hbm, cs_ref),
                (cf_hbm, cf_ref),
                (skip_hbm, skip_ref),
                (gain_hbm, gain_ref),
            ]
        )
    ]
    for copy in small:
        copy.start()
    sio_in.start()

    @pl.loop(0, NG)
    def _(g):
        feat_in(g).start()

    bar = pltpu.get_barrier_semaphore()

    @pl.loop(1, nc, unroll=5)
    def _(k):
        pl.semaphore_signal(bar, inc=1, device_id={"ctx": rank(k)}, device_id_type=MESH)

    @pl.loop(1, nh, unroll=7)
    def _(k):
        pl.semaphore_signal(bar, inc=1, device_id={"head": peer(k)}, device_id_type=MESH)


    def halo_copy(g):
        cols = pl.ds(pl.multiple_of(g * GW, GW), GW)
        return pltpu.make_async_remote_copy(
            src_ref=feat_hbm.at[pl.ds(TOK - PAD, PAD), cols],
            dst_ref=feat.at[g, pl.ds(0, PAD)],
            send_sem=halo_send.at[g],
            recv_sem=halo_recv.at[g],
            device_id={"ctx": nxt},
            device_id_type=MESH,
        )

    halo_map = pltpu.make_async_remote_copy(
        src_ref=sio_hbm.at[pl.ds(TOK - PAD, PAD)],
        dst_ref=sio.at[pl.ds(0, PAD)],
        send_sem=halo_send.at[NG],
        recv_sem=halo_recv.at[NG],
        device_id={"ctx": nxt},
        device_id_type=MESH,
    )

    pl.semaphore_wait(bar, nc - 1 + nh - 1)
    halo_map.start()

    @pl.loop(0, NG)
    def _(g):
        halo_copy(g).start()

    for copy in small:
        copy.wait()

    def four(v):
        return jnp.concatenate([v, v, v, v], axis=0)

    decay3 = [four(p.astype(F32)).astype(BF16) for p in split3(decay_ref[...])]
    step3 = [four(p.astype(F32)).astype(BF16) for p in split3(step_ref[...])]

    row = lax.broadcasted_iota(jnp.int32, (64, TOK), 0)
    tok = lax.broadcasted_iota(jnp.int32, (64, TOK), 1)
    kind, unit = row // 8, row % 8
    chunk = row % 16
    late = tok % BLK >= L // 2 + L * (chunk % 2)
    own = tok // BLK == chunk // 2
    whole = tok // BLK == unit
    middle = (tok % BLK >= L // 2) & (tok % BLK < L // 2 + L)
    hit = jnp.where((kind < 2) & own, jnp.where(late, 0.0, 1.0), 0.0)
    hit = hit + jnp.where((kind >= 2) & (kind < 4) & own & late, 1.0, 0.0)
    hit = hit + jnp.where((kind == 4) & whole, 1.0, 0.0)
    hit = hit + jnp.where((kind == 5) & whole & middle, 1.0, 0.0)
    hit = hit + jnp.where(kind == 6, 1.0, 0.0)
    hit = hit + jnp.where((kind == 7) & (tok // BLK > unit), 1.0, 0.0)
    select = hit.astype(BF16)
    sums = dot_nt(select, decay3[0]) + dot_nt(select, decay3[1]) + dot_nt(select, decay3[2])
    rows_fac[...] = split_lanes(jnp.exp(sums[0:56]))

    r = lax.broadcasted_iota(jnp.int32, (BLK, BLK), 0)
    c = lax.broadcasted_iota(jnp.int32, (BLK, BLK), 1)
    eye = jnp.where(r == c, 1.0, 0.0).astype(BF16)
    after = jnp.where(c > r, 1.0, 0.0).astype(BF16)
    for b in range(NB):
        cut = slice(b * BLK, (b + 1) * BLK)
        suffix = sums[56 + b : 57 + b]
        steps = 0.0
        for d3, s3 in zip(decay3, step3):
            suffix = suffix + dot_nt(after, d3[:, cut])
            steps = steps + dot_nt(eye, s3[:, cut])
        fac_w[cut, :] = split_lanes(jnp.exp(suffix) * steps)

    head = lax.broadcasted_iota(jnp.int32, (HEADS, CH), 0)
    chan = lax.broadcasted_iota(jnp.int32, (HEADS, CH), 1)
    widen = jnp.where(chan // HD == head, 1.0, 0.0).astype(BF16)

    def widened(v):
        hi, mid, low = split3(v)
        return dot(hi, widen) + dot(mid, widen) + dot(low, widen)

    dsend[0] = widened(jnp.exp(sums[48:56, 0:HEADS]))[0:1]
    skip_row[...] = widened(jnp.broadcast_to(skip_ref[...], (8, HEADS)))[0:1]

    def d_copy(k):
        return pltpu.make_async_remote_copy(
            src_ref=dsend.at[0],
            dst_ref=dall.at[me],
            send_sem=d_send_sem,
            recv_sem=d_recv_sem,
            device_id={"ctx": rank(k)},
            device_id_type=MESH,
        )

    d_own = pltpu.make_async_copy(dsend.at[0], dall.at[me], d_recv_sem)
    d_own.start()

    @pl.loop(1, nc, unroll=5)
    def _(k):
        d_copy(k).start()

    sr = lax.broadcasted_iota(jnp.int32, (BLK, BLK + PAD), 0)
    sc = lax.broadcasted_iota(jnp.int32, (BLK, BLK + PAD), 1)
    for k in range(TAPS - 1):
        shift[k] = jnp.where(sc == sr + PAD - TAPS + 1 + k, 1.0, 0.0).astype(BF16)

    def conv(block, taps):
        total = taps[TAPS - 1 : TAPS] * block[PAD:, :].astype(F32)
        for k in range(TAPS - 1):
            total = total + taps[k : k + 1] * dot(shift[k], block)
        return silu(total)

    def maps(i, store, blocks):
        taps = cs_ref[...].astype(F32)[:, i]
        for b in blocks:
            store(b, conv(sio[b * BLK : b * BLK + BLK + PAD, i, :], taps))

    def store_in(b, v):
        low = v.astype(BF16)
        in_rows[b * BLK : (b + 1) * BLK, :] = low
        turned = low.astype(F32).T.astype(BF16)
        in_t4[:, b * BLK : (b + 1) * BLK] = turned

    def store_out(b, v):
        out_rows[b * BLK : (b + 1) * BLK, :] = v.astype(BF16)

    sio_in.wait()
    maps(0, store_in, range(1, NB))
    halo_map.wait()

    @pl.when(me == 0)
    def _():
        sio[0:PAD] = jnp.zeros((PAD, 2, ST), BF16)

    maps(0, store_in, range(1))

    def s_copy(g, k):
        return pltpu.make_async_remote_copy(
            src_ref=sbuf.at[g, rank(k)],
            dst_ref=gath.at[g, me],
            send_sem=s_send.at[g],
            recv_sem=s_recv.at[g],
            device_id={"ctx": rank(k)},
            device_id_type=MESH,
        )

    def p_copy(g, k):
        return pltpu.make_async_remote_copy(
            src_ref=pbuf.at[g, rank(k)],
            dst_ref=inc.at[g, me],
            send_sem=p_send.at[g],
            recv_sem=p_recv.at[g],
            device_id={"ctx": rank(k)},
            device_id_type=MESH,
        )

    def z_own(g):
        return pltpu.make_async_copy(zsend.at[g, mh], z_out.at[g, mh], z_recv.at[g])

    def z_copy(g, to):
        return pltpu.make_async_remote_copy(
            src_ref=zsend.at[g, to],
            dst_ref=z_out.at[g, mh],
            send_sem=z_send.at[g],
            recv_sem=z_recv.at[g],
            device_id={"head": to},
            device_id_type=MESH,
        )

    def phase_a(g):
        feat_in(g).wait()
        spread = expander(g, 0)
        cols = pl.ds(pl.multiple_of(g * GW, GW), GW)
        taps = cf_ref[:, cols].astype(F32)

        def one(b):
            cut = slice(b * BLK, (b + 1) * BLK)
            x = conv(feat[g, b * BLK : b * BLK + BLK + PAD, :], taps).astype(BF16)
            xbuf[g, cut, :] = x
            wx[cut, :] = (dot(fac_w[cut, :], spread) * x.astype(F32)).astype(BF16)

        for b in range(1, NB):
            one(b)
        halo_copy(g).wait()

        @pl.when(me == 0)
        def _():
            feat[g, 0:PAD, :] = jnp.zeros((PAD, GW), BF16)

        one(0)
        state = dot(in_t4[...], wx[...])
        sbuf[g] = state.astype(BF16).reshape(nc, sl, GW)
        pltpu.make_async_copy(sbuf.at[g, me], gath.at[g, me], s_recv.at[g]).start()

        @pl.loop(1, nc, unroll=5)
        def _(k):
            s_copy(g, k).start()

    def prepare_b():
        maps(1, store_out, range(NB))
        inside = r // L == c // L
        mid = L // 2 - 1
        plus = inside & (c % L > mid) & (c <= r)
        minus = inside & (c % L <= mid) & (c > r)
        gap = (jnp.where(plus, 1.0, 0.0) - jnp.where(minus, 1.0, 0.0)).astype(BF16)
        lane = lax.broadcasted_iota(jnp.int32, (BLK, BLK), 1)
        for b in range(NB):
            cut = slice(b * BLK, (b + 1) * BLK)
            diff, steps = 0.0, 0.0
            for d3, s3 in zip(decay3, step3):
                diff = diff + dot_nt(gap, d3[:, cut])
                steps = steps + dot_nt(eye, s3[:, cut])
            first = lane < 2 * HEADS
            both = jnp.exp(jnp.where(first, diff, -diff)) * jnp.where(first, 1.0, steps)
            fac_ab[cut, :] = split_lanes(both)
        for n in range(NB):
            cut = slice(n * BLK, (n + 1) * BLK)
            scores = dot_nt(out_rows[cut, :], in_rows[cut, :])
            smask[n] = jnp.where(c <= r, scores, 0.0).astype(BF16)
        acc[...] = jnp.zeros_like(acc)
        whole = dall.at[pl.ds(0, nc)]
        pltpu.make_async_copy(whole, whole, d_recv_sem).wait()

    def phase_x(g):
        pltpu.make_async_copy(gath.at[g], gath.at[g], s_recv.at[g]).wait()
        cols = pl.ds(pl.multiple_of(g * GW, GW), GW)
        running = jnp.zeros((sl, GW), F32)
        for q in range(nc):
            pbuf[g, q] = running.astype(BF16)
            running = dall[q, :, cols] * running + gath[g, q].astype(F32)
        pltpu.make_async_copy(pbuf.at[g, me], inc.at[g, me], p_recv.at[g]).start()

        @pl.loop(1, nc, unroll=5)
        def _(k):
            p_copy(g, k).start()

    def phase_b(g):
        spread_a, spread_b = expander(g, 0), expander(g, 1)
        cols = pl.ds(pl.multiple_of(g * GW, GW), GW)
        skip = skip_row[:, cols]
        gain = gain_ref[:, cols]
        rows_g[...] = dot(rows_fac[...], spread_a)
        gate_in(g).wait()
        pltpu.make_async_copy(inc.at[g], inc.at[g], p_recv.at[g]).wait()
        carry[...] = inc[g].reshape(ST, GW).astype(F32)

        def one(n):
            r0 = pl.multiple_of(n * BLK, BLK)

            def factor(i):
                return rows_g[pl.ds(i, 1), :]

            fac = fac_ab[pl.ds(r0, BLK), :]
            x = xbuf[g, pl.ds(r0, BLK), :].astype(F32)
            both = dot(fac, spread_b) * x
            early, late = both[0:L], both[L:BLK]
            to_late = jnp.concatenate([early * factor(40 + n), late], axis=0)
            to_end = jnp.concatenate(
                [early * factor(16 + 2 * n), late * factor(17 + 2 * n)], axis=0
            )
            held = carry[...]
            carried = dot(out_rows[pl.ds(r0, BLK), :], held.astype(BF16))
            added = dot(in_t4[:, pl.ds(r0, BLK)], to_end.astype(BF16))
            carry[...] = held * factor(32 + n) + added
            y = jnp.concatenate(
                [
                    dot(smask[n, 0:L, 0:L], early.astype(BF16)) + carried[0:L] * factor(2 * n),
                    dot(smask[n, L:BLK, :], to_late.astype(BF16))
                    + carried[L:BLK] * factor(2 * n + 1),
                ],
                axis=0,
            )
            mixed = dot(fac, spread_a) * y + skip * x
            gated = mixed * silu(gate[g, pl.ds(r0, BLK), :].astype(F32))
            square = gated * gated
            acc[pl.ds(r0, BLK), :] += square[:, 0:128] + square[:, 128:256]
            per = tb // BLK
            zsend[g, n // per, pl.ds(pl.multiple_of((n % per) * BLK, BLK), BLK), :] = (
                gated * gain
            ).astype(BF16)

        half = nh // 2
        for part in range(2):
            pl.loop(part * NB // 2, (part + 1) * NB // 2, unroll=4)(one)

            @pl.loop(0, half, unroll=half)
            def _(k):
                to = part * half + lax.rem(mh + 1 + k, half)

                @pl.when(to == mh)
                def _():
                    z_own(g).start()

                @pl.when(to != mh)
                def _():
                    z_copy(g, to).start()

    def states_by(i):
        return jnp.clip(jnp.maximum(i + 1, 2 * i - 1), 0, NG)

    def prefixes_by(i):
        return jnp.clip(jnp.maximum(i, 2 * i - 3), 0, NG)

    @pl.loop(0, NG + 2)
    def _(i):
        pl.loop(states_by(i - 1), states_by(i))(phase_a)

        @pl.when(i == 1)
        def _():
            @pl.loop(0, NG)
            def _(g):
                gate_in(g).start()

            prepare_b()

        pl.loop(prefixes_by(i - 1), prefixes_by(i))(phase_x)

        @pl.when(i >= 2)
        def _():
            phase_b(i - 2)

    for b in range(NB):
        flat = jnp.sum(acc[b * BLK : (b + 1) * BLK, :].T, axis=0, keepdims=True)
        unit, part = b * BLK // tb, b * BLK % tb
        rs_send[unit, :, part : part + BLK] = lax.rsqrt(flat * (1.0 / CH) + 1e-05)
    pltpu.make_async_copy(rs_send.at[mh], rs_out.at[mh], r_recv).start()

    def r_copy(k):
        return pltpu.make_async_remote_copy(
            src_ref=rs_send.at[peer(k)],
            dst_ref=rs_out.at[mh],
            send_sem=r_send,
            recv_sem=r_recv,
            device_id={"head": peer(k)},
            device_id_type=MESH,
        )

    @pl.loop(1, nh, unroll=7)
    def _(k):
        r_copy(k).start()

    some = dall.at[pl.ds(0, nc - 1)]
    pltpu.make_async_copy(some, some, d_send_sem).wait()

    @pl.loop(0, NG)
    def _(g):
        part = gath.at[g, pl.ds(0, nc - 1)]
        pltpu.make_async_copy(part, part, s_send.at[g]).wait()
        pltpu.make_async_copy(part, part, p_send.at[g]).wait()
        piece = zsend.at[g, pl.ds(0, nh - 1)]
        pltpu.make_async_copy(piece, piece, z_send.at[g]).wait()

    @pl.loop(0, NG)
    def _(g):
        pltpu.make_async_copy(zsend.at[g], zsend.at[g], z_recv.at[g]).wait()

    part = rs_send.at[pl.ds(0, nh - 1)]
    pltpu.make_async_copy(part, part, r_send).wait()
    pltpu.make_async_copy(rs_send, rs_send, r_recv).wait()


def mixer(nc, nh, *args):
    sl, tb = ST // nc, TOK // nh
    any_spec = pl.BlockSpec(memory_space=pl.ANY)
    hbm = pl.BlockSpec(memory_space=pltpu.HBM)
    dma = pltpu.SemaphoreType.DMA
    return pl.pallas_call(
        functools.partial(mixer_kernel, nc, nh),
        out_shape=[
            jax.ShapeDtypeStruct((NG, nh, tb, GW), BF16),
            jax.ShapeDtypeStruct((nh, 1, tb), F32),
        ],
        in_specs=[any_spec] * 3 + [hbm] * 6,
        out_specs=[any_spec, any_spec],
        scratch_shapes=[
            pltpu.VMEM((HEADS, TOK), F32),
            pltpu.VMEM((HEADS, TOK), F32),
            pltpu.VMEM((TAPS, CH), BF16),
            pltpu.VMEM((TAPS, 2, ST), BF16),
            pltpu.VMEM((1, HEADS), F32),
            pltpu.VMEM((1, CH), F32),
            pltpu.VMEM((1, CH), F32),
            pltpu.VMEM((NG, TOK + PAD, GW), BF16),
            pltpu.VMEM((NG, TOK, GW), BF16),
            pltpu.VMEM((TOK + PAD, 2, ST), BF16),
            pltpu.VMEM((NG, TOK, GW), BF16),
            pltpu.VMEM((TOK, GW), BF16),
            pltpu.VMEM((TOK, ST), BF16),
            pltpu.VMEM((TOK, ST), BF16),
            pltpu.VMEM((ST, TOK), BF16),
            pltpu.VMEM((NB, BLK, BLK), BF16),
            pltpu.VMEM((TOK, 128), BF16),
            pltpu.VMEM((TOK, 128), BF16),
            pltpu.VMEM((56, 128), BF16),
            pltpu.VMEM((56, GW), F32),
            pltpu.VMEM((TAPS - 1, BLK, BLK + PAD), BF16),
            pltpu.VMEM((TOK, 128), F32),
            pltpu.VMEM((ST, GW), F32),
            pltpu.VMEM((NG, nc, sl, GW), BF16),
            pltpu.VMEM((NG, nc, sl, GW), BF16),
            pltpu.VMEM((NG, nc, sl, GW), BF16),
            pltpu.VMEM((NG, nc, sl, GW), BF16),
            pltpu.VMEM((1, 1, CH), F32),
            pltpu.VMEM((nc, 1, CH), F32),
            pltpu.VMEM((NG, nh, tb, GW), BF16),
            pltpu.VMEM((nh, 1, tb), F32),
            dma((6,)),
            dma((NG,)),
            dma((NG,)),
            dma,
            dma((NG + 1,)),
            dma((NG + 1,)),
            dma,
            dma,
            dma((NG,)),
            dma((NG,)),
            dma((NG,)),
            dma((NG,)),
            dma((NG,)),
            dma((NG,)),
            dma,
            dma,
        ],
        compiler_params=pltpu.CompilerParams(
            collective_id=0, has_side_effects=True, vmem_limit_bytes=56 << 20
        ),
        cost_estimate=pl.CostEstimate(
            flops=6_000_000_000, bytes_accessed=16_000_000, transcendentals=5_000_000
        ),
    )(*args)


def norm_kernel(z_hbm, rs_hbm, o_hbm, zin, rs, stage, in_sem, rs_sem, out_sem):
    nh, tb = z_hbm.shape[1], z_hbm.shape[2]

    def into(j):
        return pltpu.make_async_copy(z_hbm.at[:, j], zin.at[j], in_sem.at[j])

    def out(j):
        cols = pl.ds(pl.multiple_of(j * CH, CH), CH)
        return pltpu.make_async_copy(stage.at[j], o_hbm.at[:, cols], out_sem.at[j])

    factors = pltpu.make_async_copy(rs_hbm, rs, rs_sem)
    factors.start()

    @pl.loop(0, nh)
    def _(j):
        into(j).start()

    factors.wait()

    @pl.loop(0, nh)
    def _(j):
        col = jnp.broadcast_to(rs[j], (128, tb)).T
        into(j).wait()
        for g in range(NG):
            for half in range(GW // 128):
                low = half * 128
                z = zin[j, g, :, low : low + 128].astype(F32)
                stage[j, :, g * GW + low : g * GW + low + 128] = (z * col).astype(BF16)
        out(j).start()

    @pl.loop(0, nh)
    def _(j):
        out(j).wait()


def normalize(nh, z, rs):
    tb = TOK // nh
    hbm = pl.BlockSpec(memory_space=pltpu.HBM)
    dma = pltpu.SemaphoreType.DMA
    return pl.pallas_call(
        norm_kernel,
        out_shape=jax.ShapeDtypeStruct((tb, nh * CH), BF16),
        in_specs=[hbm, hbm],
        out_specs=hbm,
        scratch_shapes=[
            pltpu.VMEM((nh, NG, tb, GW), BF16),
            pltpu.VMEM((nh, 1, tb), F32),
            pltpu.VMEM((nh, tb, CH), BF16),
            dma((nh,)),
            dma,
            dma((nh,)),
        ],
        compiler_params=pltpu.CompilerParams(vmem_limit_bytes=56 << 20),
        cost_estimate=pl.CostEstimate(
            flops=4_000_000, bytes_accessed=8_400_000, transcendentals=0
        ),
    )(z, rs)


def shards(
    features, gates, state_io, step_size, log_decay, conv_feat, conv_state, skip_gain, norm_gain
):
    nc, nh = lax.axis_size("ctx"), lax.axis_size("head")
    z, rs = mixer(
        nc,
        nh,
        features,
        gates,
        state_io,
        step_size,
        log_decay,
        conv_feat,
        conv_state,
        skip_gain.reshape(1, HEADS),
        norm_gain.reshape(1, CH),
    )
    return normalize(nh, z, rs)


def solution(mesh):
    in_specs = (
        P("ctx", "head"),
        P("ctx", "head"),
        P("ctx", None, "head"),
        P("head", "ctx"),
        P("head", "ctx"),
        P(None, "head"),
        P(None, None, "head"),
        P("head"),
        P("head"),
    )
    out_specs = P(("ctx", "head"), None)
    return jax.shard_map(shards, mesh=mesh, in_specs=in_specs, out_specs=out_specs, check_vma=False)
```

```python
import functools

import jax
import jax.numpy as jnp
from jax import lax
from jax.experimental import pallas as pl
from jax.experimental.pallas import tpu as pltpu
from jax.sharding import PartitionSpec as P

F32 = jnp.float32
BF16 = jnp.bfloat16
MESH = pl.DeviceIdType.MESH

TOK = 1024
CH = 2048
HEADS = 32
HD = 64
ST = 256
GW = 256
NG = CH // GW
PER = GW // HD
L = 64
BLK = 128
NB = TOK // BLK
PAD = 16
TAPS = 4


def dot(a, b):
    return jnp.dot(a, b, preferred_element_type=F32)


def dot_nt(a, b):
    return lax.dot_general(a, b, (((1,), (1,)), ((), ())), preferred_element_type=F32)


def silu(v):
    half = 0.5 * v
    return half + half * jnp.tanh(half)


def split3(v):
    hi = v.astype(BF16)
    rest = v - hi.astype(F32)
    mid = rest.astype(BF16)
    low = (rest - mid.astype(F32)).astype(BF16)
    return hi, mid, low


def split_lanes(v):
    hi = v.astype(BF16).astype(F32)
    lane = lax.broadcasted_iota(jnp.int32, v.shape, 1)
    return jnp.where((lane // HEADS) % 2 == 0, hi, v - hi).astype(BF16)


def expander(piece, part):
    row = lax.broadcasted_iota(jnp.int32, (4 * HEADS, GW), 0)
    col = lax.broadcasted_iota(jnp.int32, (4 * HEADS, GW), 1)
    hit = (row % HEADS == PER * piece + col // HD) & (row // (2 * HEADS) == part)
    return jnp.where(hit, 1.0, 0.0).astype(BF16)


def mixer_kernel(
    nc,
    nh,
    feat_hbm,
    gate_hbm,
    sio_hbm,
    step_hbm,
    decay_hbm,
    cf_hbm,
    cs_hbm,
    skip_hbm,
    gain_hbm,
    z_out,
    rs_out,
    step_ref,
    decay_ref,
    cf_ref,
    cs_ref,
    skip_ref,
    gain_ref,
    skip_row,
    feat,
    gate,
    sio,
    xbuf,
    wx,
    in_rows,
    out_rows,
    in_t4,
    smask,
    fac_ab,
    fac_w,
    rows_fac,
    rows_g,
    shift,
    acc,
    carry,
    sbuf,
    gath,
    pbuf,
    inc,
    dsend,
    dall,
    zsend,
    rs_send,
    small_sem,
    feat_sem,
    gate_sem,
    sio_sem,
    halo_send,
    halo_recv,
    d_send_sem,
    d_recv_sem,
    s_send,
    s_recv,
    p_send,
    p_recv,
    z_send,
    z_recv,
    r_send,
    r_recv,
):
    me = lax.axis_index("ctx")
    mh = lax.axis_index("head")
    sl = ST // nc
    tb = TOK // nh
    nxt = lax.rem(me + 1, nc)

    def rank(k):
        return lax.rem(me + k, nc)

    def peer(k):
        return lax.rem(mh + k, nh)

    sio_in = pltpu.make_async_copy(sio_hbm, sio.at[pl.ds(PAD, TOK)], sio_sem)

    def feat_in(g):
        cols = pl.ds(pl.multiple_of(g * GW, GW), GW)
        return pltpu.make_async_copy(
            feat_hbm.at[:, cols], feat.at[g, pl.ds(PAD, TOK)], feat_sem.at[g]
        )

    def gate_in(g):
        cols = pl.ds(pl.multiple_of(g * GW, GW), GW)
        return pltpu.make_async_copy(gate_hbm.at[:, cols], gate.at[g], gate_sem.at[g])

    small = [
        pltpu.make_async_copy(source, target, small_sem.at[i])
        for i, (source, target) in enumerate(
            [
                (decay_hbm, decay_ref),
                (step_hbm, step_ref),
                (cs_hbm, cs_ref),
                (cf_hbm, cf_ref),
                (skip_hbm, skip_ref),
                (gain_hbm, gain_ref),
            ]
        )
    ]
    for copy in small:
        copy.start()
    sio_in.start()

    @pl.loop(0, NG)
    def _(g):
        feat_in(g).start()

    bar = pltpu.get_barrier_semaphore()

    @pl.loop(1, nc, unroll=5)
    def _(k):
        pl.semaphore_signal(bar, inc=1, device_id={"ctx": rank(k)}, device_id_type=MESH)

    @pl.loop(1, nh, unroll=7)
    def _(k):
        pl.semaphore_signal(bar, inc=1, device_id={"head": peer(k)}, device_id_type=MESH)


    def halo_copy(g):
        cols = pl.ds(pl.multiple_of(g * GW, GW), GW)
        return pltpu.make_async_remote_copy(
            src_ref=feat_hbm.at[pl.ds(TOK - PAD, PAD), cols],
            dst_ref=feat.at[g, pl.ds(0, PAD)],
            send_sem=halo_send.at[g],
            recv_sem=halo_recv.at[g],
            device_id={"ctx": nxt},
            device_id_type=MESH,
        )

    halo_map = pltpu.make_async_remote_copy(
        src_ref=sio_hbm.at[pl.ds(TOK - PAD, PAD)],
        dst_ref=sio.at[pl.ds(0, PAD)],
        send_sem=halo_send.at[NG],
        recv_sem=halo_recv.at[NG],
        device_id={"ctx": nxt},
        device_id_type=MESH,
    )

    pl.semaphore_wait(bar, nc - 1 + nh - 1)
    halo_map.start()

    @pl.loop(0, NG)
    def _(g):
        halo_copy(g).start()

    for copy in small:
        copy.wait()

    def four(v):
        return jnp.concatenate([v, v, v, v], axis=0)

    decay3 = [four(p.astype(F32)).astype(BF16) for p in split3(decay_ref[...])]
    step3 = [four(p.astype(F32)).astype(BF16) for p in split3(step_ref[...])]

    row = lax.broadcasted_iota(jnp.int32, (64, TOK), 0)
    tok = lax.broadcasted_iota(jnp.int32, (64, TOK), 1)
    kind, unit = row // 8, row % 8
    chunk = row % 16
    late = tok % BLK >= L // 2 + L * (chunk % 2)
    own = tok // BLK == chunk // 2
    whole = tok // BLK == unit
    middle = (tok % BLK >= L // 2) & (tok % BLK < L // 2 + L)
    hit = jnp.where((kind < 2) & own, jnp.where(late, 0.0, 1.0), 0.0)
    hit = hit + jnp.where((kind >= 2) & (kind < 4) & own & late, 1.0, 0.0)
    hit = hit + jnp.where((kind == 4) & whole, 1.0, 0.0)
    hit = hit + jnp.where((kind == 5) & whole & middle, 1.0, 0.0)
    hit = hit + jnp.where(kind == 6, 1.0, 0.0)
    hit = hit + jnp.where((kind == 7) & (tok // BLK > unit), 1.0, 0.0)
    select = hit.astype(BF16)
    sums = dot_nt(select, decay3[0]) + dot_nt(select, decay3[1]) + dot_nt(select, decay3[2])
    rows_fac[...] = split_lanes(jnp.exp(sums[0:56]))

    r = lax.broadcasted_iota(jnp.int32, (BLK, BLK), 0)
    c = lax.broadcasted_iota(jnp.int32, (BLK, BLK), 1)
    eye = jnp.where(r == c, 1.0, 0.0).astype(BF16)
    after = jnp.where(c > r, 1.0, 0.0).astype(BF16)
    for b in range(NB):
        cut = slice(b * BLK, (b + 1) * BLK)
        suffix = sums[56 + b : 57 + b]
        steps = 0.0
        for d3, s3 in zip(decay3, step3):
            suffix = suffix + dot_nt(after, d3[:, cut])
            steps = steps + dot_nt(eye, s3[:, cut])
        fac_w[cut, :] = split_lanes(jnp.exp(suffix) * steps)

    head = lax.broadcasted_iota(jnp.int32, (HEADS, CH), 0)
    chan = lax.broadcasted_iota(jnp.int32, (HEADS, CH), 1)
    widen = jnp.where(chan // HD == head, 1.0, 0.0).astype(BF16)

    def widened(v):
        hi, mid, low = split3(v)
        return dot(hi, widen) + dot(mid, widen) + dot(low, widen)

    dsend[0] = widened(jnp.exp(sums[48:56, 0:HEADS]))[0:1]
    skip_row[...] = widened(jnp.broadcast_to(skip_ref[...], (8, HEADS)))[0:1]

    def d_copy(k):
        return pltpu.make_async_remote_copy(
            src_ref=dsend.at[0],
            dst_ref=dall.at[me],
            send_sem=d_send_sem,
            recv_sem=d_recv_sem,
            device_id={"ctx": rank(k)},
            device_id_type=MESH,
        )

    d_own = pltpu.make_async_copy(dsend.at[0], dall.at[me], d_recv_sem)
    d_own.start()

    @pl.loop(1, nc, unroll=5)
    def _(k):
        d_copy(k).start()

    sr = lax.broadcasted_iota(jnp.int32, (BLK, BLK + PAD), 0)
    sc = lax.broadcasted_iota(jnp.int32, (BLK, BLK + PAD), 1)
    for k in range(TAPS - 1):
        shift[k] = jnp.where(sc == sr + PAD - TAPS + 1 + k, 1.0, 0.0).astype(BF16)

    def conv(block, taps):
        total = taps[TAPS - 1 : TAPS] * block[PAD:, :].astype(F32)
        for k in range(TAPS - 1):
            total = total + taps[k : k + 1] * dot(shift[k], block)
        return silu(total)

    def maps(i, store, blocks):
        taps = cs_ref[...].astype(F32)[:, i]
        for b in blocks:
            store(b, conv(sio[b * BLK : b * BLK + BLK + PAD, i, :], taps))

    def store_in(b, v):
        low = v.astype(BF16)
        in_rows[b * BLK : (b + 1) * BLK, :] = low
        turned = low.astype(F32).T.astype(BF16)
        in_t4[:, b * BLK : (b + 1) * BLK] = turned

    def store_out(b, v):
        out_rows[b * BLK : (b + 1) * BLK, :] = v.astype(BF16)

    sio_in.wait()
    maps(0, store_in, range(1, NB))
    halo_map.wait()

    @pl.when(me == 0)
    def _():
        sio[0:PAD] = jnp.zeros((PAD, 2, ST), BF16)

    maps(0, store_in, range(1))

    def s_copy(g, k):
        return pltpu.make_async_remote_copy(
            src_ref=sbuf.at[g, rank(k)],
            dst_ref=gath.at[g, me],
            send_sem=s_send.at[g],
            recv_sem=s_recv.at[g],
            device_id={"ctx": rank(k)},
            device_id_type=MESH,
        )

    def p_copy(g, k):
        return pltpu.make_async_remote_copy(
            src_ref=pbuf.at[g, rank(k)],
            dst_ref=inc.at[g, me],
            send_sem=p_send.at[g],
            recv_sem=p_recv.at[g],
            device_id={"ctx": rank(k)},
            device_id_type=MESH,
        )

    def z_own(g):
        return pltpu.make_async_copy(zsend.at[g, mh], z_out.at[g, mh], z_recv.at[g])

    def z_copy(g, to):
        return pltpu.make_async_remote_copy(
            src_ref=zsend.at[g, to],
            dst_ref=z_out.at[g, mh],
            send_sem=z_send.at[g],
            recv_sem=z_recv.at[g],
            device_id={"head": to},
            device_id_type=MESH,
        )

    def phase_a(g):
        feat_in(g).wait()
        spread = expander(g, 0)
        cols = pl.ds(pl.multiple_of(g * GW, GW), GW)
        taps = cf_ref[:, cols].astype(F32)

        def one(b):
            cut = slice(b * BLK, (b + 1) * BLK)
            x = conv(feat[g, b * BLK : b * BLK + BLK + PAD, :], taps).astype(BF16)
            xbuf[g, cut, :] = x
            wx[cut, :] = (dot(fac_w[cut, :], spread) * x.astype(F32)).astype(BF16)

        for b in range(1, NB):
            one(b)
        halo_copy(g).wait()

        @pl.when(me == 0)
        def _():
            feat[g, 0:PAD, :] = jnp.zeros((PAD, GW), BF16)

        one(0)
        state = dot(in_t4[...], wx[...])
        sbuf[g] = state.astype(BF16).reshape(nc, sl, GW)
        pltpu.make_async_copy(sbuf.at[g, me], gath.at[g, me], s_recv.at[g]).start()

        @pl.loop(1, nc, unroll=5)
        def _(k):
            s_copy(g, k).start()

    def prepare_b():
        maps(1, store_out, range(NB))
        inside = r // L == c // L
        mid = L // 2 - 1
        plus = inside & (c % L > mid) & (c <= r)
        minus = inside & (c % L <= mid) & (c > r)
        gap = (jnp.where(plus, 1.0, 0.0) - jnp.where(minus, 1.0, 0.0)).astype(BF16)
        lane = lax.broadcasted_iota(jnp.int32, (BLK, BLK), 1)
        for b in range(NB):
            cut = slice(b * BLK, (b + 1) * BLK)
            diff, steps = 0.0, 0.0
            for d3, s3 in zip(decay3, step3):
                diff = diff + dot_nt(gap, d3[:, cut])
                steps = steps + dot_nt(eye, s3[:, cut])
            first = lane < 2 * HEADS
            both = jnp.exp(jnp.where(first, diff, -diff)) * jnp.where(first, 1.0, steps)
            fac_ab[cut, :] = split_lanes(both)
        for n in range(NB):
            cut = slice(n * BLK, (n + 1) * BLK)
            scores = dot_nt(out_rows[cut, :], in_rows[cut, :])
            smask[n] = jnp.where(c <= r, scores, 0.0).astype(BF16)
        acc[...] = jnp.zeros_like(acc)
        whole = dall.at[pl.ds(0, nc)]
        pltpu.make_async_copy(whole, whole, d_recv_sem).wait()

    def phase_x(g):
        pltpu.make_async_copy(gath.at[g], gath.at[g], s_recv.at[g]).wait()
        cols = pl.ds(pl.multiple_of(g * GW, GW), GW)
        running = jnp.zeros((sl, GW), F32)
        for q in range(nc):
            pbuf[g, q] = running.astype(BF16)
            running = dall[q, :, cols] * running + gath[g, q].astype(F32)
        pltpu.make_async_copy(pbuf.at[g, me], inc.at[g, me], p_recv.at[g]).start()

        @pl.loop(1, nc, unroll=5)
        def _(k):
            p_copy(g, k).start()

    def phase_b(g):
        spread_a, spread_b = expander(g, 0), expander(g, 1)
        cols = pl.ds(pl.multiple_of(g * GW, GW), GW)
        skip = skip_row[:, cols]
        gain = gain_ref[:, cols]
        rows_g[...] = dot(rows_fac[...], spread_a)
        gate_in(g).wait()
        pltpu.make_async_copy(inc.at[g], inc.at[g], p_recv.at[g]).wait()
        carry[...] = inc[g].reshape(ST, GW).astype(F32)

        def one(n):
            r0 = pl.multiple_of(n * BLK, BLK)

            def factor(i):
                return rows_g[pl.ds(i, 1), :]

            fac = fac_ab[pl.ds(r0, BLK), :]
            x = xbuf[g, pl.ds(r0, BLK), :].astype(F32)
            both = dot(fac, spread_b) * x
            early, late = both[0:L], both[L:BLK]
            to_late = jnp.concatenate([early * factor(40 + n), late], axis=0)
            to_end = jnp.concatenate(
                [early * factor(16 + 2 * n), late * factor(17 + 2 * n)], axis=0
            )
            held = carry[...]
            carried = dot(out_rows[pl.ds(r0, BLK), :], held.astype(BF16))
            added = dot(in_t4[:, pl.ds(r0, BLK)], to_end.astype(BF16))
            carry[...] = held * factor(32 + n) + added
            y = jnp.concatenate(
                [
                    dot(smask[n, 0:L, 0:L], early.astype(BF16)) + carried[0:L] * factor(2 * n),
                    dot(smask[n, L:BLK, :], to_late.astype(BF16))
                    + carried[L:BLK] * factor(2 * n + 1),
                ],
                axis=0,
            )
            mixed = dot(fac, spread_a) * y + skip * x
            gated = mixed * silu(gate[g, pl.ds(r0, BLK), :].astype(F32))
            square = gated * gated
            acc[pl.ds(r0, BLK), :] += square[:, 0:128] + square[:, 128:256]
            per = tb // BLK
            zsend[g, n // per, pl.ds(pl.multiple_of((n % per) * BLK, BLK), BLK), :] = (
                gated * gain
            ).astype(BF16)

        half = nh // 4
        for part in range(4):
            pl.loop(part * NB // 4, (part + 1) * NB // 4, unroll=2)(one)

            @pl.loop(0, half, unroll=half)
            def _(k):
                to = part * half + lax.rem(mh + 1 + k, half)

                @pl.when(to == mh)
                def _():
                    z_own(g).start()

                @pl.when(to != mh)
                def _():
                    z_copy(g, to).start()

    def states_by(i):
        return jnp.clip(jnp.maximum(i + 1, 2 * i - 1), 0, NG)

    def prefixes_by(i):
        return jnp.clip(jnp.maximum(i, 2 * i - 3), 0, NG)

    @pl.loop(0, NG + 2)
    def _(i):
        pl.loop(states_by(i - 1), states_by(i))(phase_a)

        @pl.when(i == 1)
        def _():
            @pl.loop(0, NG)
            def _(g):
                gate_in(g).start()

            prepare_b()

        pl.loop(prefixes_by(i - 1), prefixes_by(i))(phase_x)

        @pl.when(i >= 2)
        def _():
            phase_b(i - 2)

    for b in range(NB):
        flat = jnp.sum(acc[b * BLK : (b + 1) * BLK, :].T, axis=0, keepdims=True)
        unit, part = b * BLK // tb, b * BLK % tb
        rs_send[unit, :, part : part + BLK] = lax.rsqrt(flat * (1.0 / CH) + 1e-05)
    pltpu.make_async_copy(rs_send.at[mh], rs_out.at[mh], r_recv).start()

    def r_copy(k):
        return pltpu.make_async_remote_copy(
            src_ref=rs_send.at[peer(k)],
            dst_ref=rs_out.at[mh],
            send_sem=r_send,
            recv_sem=r_recv,
            device_id={"head": peer(k)},
            device_id_type=MESH,
        )

    @pl.loop(1, nh, unroll=7)
    def _(k):
        r_copy(k).start()

    some = dall.at[pl.ds(0, nc - 1)]
    pltpu.make_async_copy(some, some, d_send_sem).wait()

    @pl.loop(0, NG)
    def _(g):
        part = gath.at[g, pl.ds(0, nc - 1)]
        pltpu.make_async_copy(part, part, s_send.at[g]).wait()
        pltpu.make_async_copy(part, part, p_send.at[g]).wait()
        piece = zsend.at[g, pl.ds(0, nh - 1)]
        pltpu.make_async_copy(piece, piece, z_send.at[g]).wait()

    @pl.loop(0, NG)
    def _(g):
        pltpu.make_async_copy(zsend.at[g], zsend.at[g], z_recv.at[g]).wait()

    part = rs_send.at[pl.ds(0, nh - 1)]
    pltpu.make_async_copy(part, part, r_send).wait()
    pltpu.make_async_copy(rs_send, rs_send, r_recv).wait()


def mixer(nc, nh, *args):
    sl, tb = ST // nc, TOK // nh
    any_spec = pl.BlockSpec(memory_space=pl.ANY)
    hbm = pl.BlockSpec(memory_space=pltpu.HBM)
    dma = pltpu.SemaphoreType.DMA
    return pl.pallas_call(
        functools.partial(mixer_kernel, nc, nh),
        out_shape=[
            jax.ShapeDtypeStruct((NG, nh, tb, GW), BF16),
            jax.ShapeDtypeStruct((nh, 1, tb), F32),
        ],
        in_specs=[any_spec] * 3 + [hbm] * 6,
        out_specs=[any_spec, any_spec],
        scratch_shapes=[
            pltpu.VMEM((HEADS, TOK), F32),
            pltpu.VMEM((HEADS, TOK), F32),
            pltpu.VMEM((TAPS, CH), BF16),
            pltpu.VMEM((TAPS, 2, ST), BF16),
            pltpu.VMEM((1, HEADS), F32),
            pltpu.VMEM((1, CH), F32),
            pltpu.VMEM((1, CH), F32),
            pltpu.VMEM((NG, TOK + PAD, GW), BF16),
            pltpu.VMEM((NG, TOK, GW), BF16),
            pltpu.VMEM((TOK + PAD, 2, ST), BF16),
            pltpu.VMEM((NG, TOK, GW), BF16),
            pltpu.VMEM((TOK, GW), BF16),
            pltpu.VMEM((TOK, ST), BF16),
            pltpu.VMEM((TOK, ST), BF16),
            pltpu.VMEM((ST, TOK), BF16),
            pltpu.VMEM((NB, BLK, BLK), BF16),
            pltpu.VMEM((TOK, 128), BF16),
            pltpu.VMEM((TOK, 128), BF16),
            pltpu.VMEM((56, 128), BF16),
            pltpu.VMEM((56, GW), F32),
            pltpu.VMEM((TAPS - 1, BLK, BLK + PAD), BF16),
            pltpu.VMEM((TOK, 128), F32),
            pltpu.VMEM((ST, GW), F32),
            pltpu.VMEM((NG, nc, sl, GW), BF16),
            pltpu.VMEM((NG, nc, sl, GW), BF16),
            pltpu.VMEM((NG, nc, sl, GW), BF16),
            pltpu.VMEM((NG, nc, sl, GW), BF16),
            pltpu.VMEM((1, 1, CH), F32),
            pltpu.VMEM((nc, 1, CH), F32),
            pltpu.VMEM((NG, nh, tb, GW), BF16),
            pltpu.VMEM((nh, 1, tb), F32),
            dma((6,)),
            dma((NG,)),
            dma((NG,)),
            dma,
            dma((NG + 1,)),
            dma((NG + 1,)),
            dma,
            dma,
            dma((NG,)),
            dma((NG,)),
            dma((NG,)),
            dma((NG,)),
            dma((NG,)),
            dma((NG,)),
            dma,
            dma,
        ],
        compiler_params=pltpu.CompilerParams(
            collective_id=0, has_side_effects=True, vmem_limit_bytes=56 << 20
        ),
        cost_estimate=pl.CostEstimate(
            flops=6_000_000_000, bytes_accessed=16_000_000, transcendentals=5_000_000
        ),
    )(*args)


def norm_kernel(z_hbm, rs_hbm, o_hbm, zin, rs, stage, in_sem, rs_sem, out_sem):
    nh, tb = z_hbm.shape[1], z_hbm.shape[2]

    def into(j):
        return pltpu.make_async_copy(z_hbm.at[:, j], zin.at[j], in_sem.at[j])

    def out(j):
        cols = pl.ds(pl.multiple_of(j * CH, CH), CH)
        return pltpu.make_async_copy(stage.at[j], o_hbm.at[:, cols], out_sem.at[j])

    factors = pltpu.make_async_copy(rs_hbm, rs, rs_sem)
    factors.start()

    @pl.loop(0, nh)
    def _(j):
        into(j).start()

    factors.wait()

    @pl.loop(0, nh)
    def _(j):
        col = jnp.broadcast_to(rs[j], (128, tb)).T
        into(j).wait()
        for g in range(NG):
            for half in range(GW // 128):
                low = half * 128
                z = zin[j, g, :, low : low + 128].astype(F32)
                stage[j, :, g * GW + low : g * GW + low + 128] = (z * col).astype(BF16)
        out(j).start()

    @pl.loop(0, nh)
    def _(j):
        out(j).wait()


def normalize(nh, z, rs):
    tb = TOK // nh
    hbm = pl.BlockSpec(memory_space=pltpu.HBM)
    dma = pltpu.SemaphoreType.DMA
    return pl.pallas_call(
        norm_kernel,
        out_shape=jax.ShapeDtypeStruct((tb, nh * CH), BF16),
        in_specs=[hbm, hbm],
        out_specs=hbm,
        scratch_shapes=[
            pltpu.VMEM((nh, NG, tb, GW), BF16),
            pltpu.VMEM((nh, 1, tb), F32),
            pltpu.VMEM((nh, tb, CH), BF16),
            dma((nh,)),
            dma,
            dma((nh,)),
        ],
        compiler_params=pltpu.CompilerParams(vmem_limit_bytes=56 << 20),
        cost_estimate=pl.CostEstimate(
            flops=4_000_000, bytes_accessed=8_400_000, transcendentals=0
        ),
    )(z, rs)


def shards(
    features, gates, state_io, step_size, log_decay, conv_feat, conv_state, skip_gain, norm_gain
):
    nc, nh = lax.axis_size("ctx"), lax.axis_size("head")
    z, rs = mixer(
        nc,
        nh,
        features,
        gates,
        state_io,
        step_size,
        log_decay,
        conv_feat,
        conv_state,
        skip_gain.reshape(1, HEADS),
        norm_gain.reshape(1, CH),
    )
    return normalize(nh, z, rs)


def solution(mesh):
    in_specs = (
        P("ctx", "head"),
        P("ctx", "head"),
        P("ctx", None, "head"),
        P("head", "ctx"),
        P("head", "ctx"),
        P(None, "head"),
        P(None, None, "head"),
        P("head"),
        P("head"),
    )
    out_specs = P(("ctx", "head"), None)
    return jax.shard_map(shards, mesh=mesh, in_specs=in_specs, out_specs=out_specs, check_vma=False)
```
